512 devices in a mesh: section: 16 (over y_hi, z), ctx: 8 (over x, core), tp: 4 (over y_lo).
Axes of the slice: x: 4, y: 8 (y_hi: 2, y_lo: 4; y = y_hi * 4 + y_lo), z: 8, core: 2. Of those that a mesh axis runs over, the one named last changes fastest.
Arguments:
- queries: bfloat16 [16, 2048, 8192], P('section', 'ctx', 'tp'), may hold values from -4.5 to 4.5
- keys: bfloat16 [16, 2048, 1024], P('section', 'ctx', 'tp'), may hold values from -4.5 to 4.5
- values: bfloat16 [16, 2048, 1024], P('section', 'ctx', 'tp'), may hold values from -6 to 6
- residual: bfloat16 [16, 2048, 8192], P('section', 'ctx', 'tp'), may hold values from -1.796875 to 1.796875
- rand_blocks: int32 [16, 16, 3], P('section'), may hold values from 0 to 15, as said below
- block_order: int32 [16, 16], P('section'), may hold values from 0 to 15, each once within a row
Outputs:
- received: bfloat16 [16, 2048, 8192], P('section', 'ctx', 'tp')
The draws below stay inside these ranges and needn't reach their ends.
Inputs may be any that keep to these rules, and one draw needn't show every extreme that they name: `rand_blocks`: query block i's entries lie in 0 to i.
All inputs are finite; a program needn't handle non-finite values.
Results may differ from the reference program's by a relative error of at most 0.0038.
Values may be sent and summed in bfloat16 or wider, within the bound.
A program may use at most 64 MiB of HBM per device.

```python
import math
import jax
import jax.numpy as jnp
from jax import lax

D = 8192
HQ = 64
KVH = 8
HD = 128
BLOCK = 128
RAND = 3
NBLK = 16
SEQ = 2048
SECTIONS = 16


def draw_queries(key, part):
    key = jax.random.fold_in(key, 3)
    complete = jnp.clip(jax.random.normal(key, (SECTIONS, SEQ, HQ, HD), jnp.float32), -4.5, 4.5)
    return complete.reshape(SECTIONS, SEQ, HQ * HD).astype(jnp.bfloat16)


def draw_keys(key, part):
    key = jax.random.fold_in(key, 5)
    complete = jnp.clip(jax.random.normal(key, (SECTIONS, SEQ, KVH, HD), jnp.float32), -4.5, 4.5)
    return complete.reshape(SECTIONS, SEQ, KVH * HD).astype(jnp.bfloat16)


def draw_rand_blocks(key, part):
    key = jax.random.fold_in(key, 7)
    raw_values = jax.random.randint(key, (SECTIONS, NBLK, RAND), 0, 1 << 20)
    upper_bound = jnp.arange(NBLK, dtype=jnp.int32)[None, :, None] + 1
    drawn = (raw_values % upper_bound).astype(jnp.int32)
    block_ids = jnp.arange(NBLK, dtype=jnp.int32)[None, :, None]
    slot_ids = jnp.arange(RAND, dtype=jnp.int32)[None, None, :]
    top_entry = (block_ids == NBLK - 1) & (slot_ids == 0)
    return jnp.where(top_entry, NBLK - 1, drawn).astype(jnp.int32)


def steps_of(key, dims, split, least, high):
    gain, own = 1.0, jax.random.fold_in(key, 6)
    for axis_at, blocks in split:
        draws = jnp.exp(jax.random.uniform(jax.random.fold_in(own, axis_at), (blocks,), jnp.float32, least / len(split), high / len(split)))
        gain = gain * jnp.repeat(draws, dims[axis_at] // blocks).reshape([-1 if axis == axis_at else 1 for axis in range(len(dims))])
    return gain


def scatter_about(key, shape, scale, reach, split=(), kind=jnp.bfloat16):
    gain = steps_of(key, shape, split, -0.22, 0.18) if split else 1.0
    result = jax.random.normal(key, shape, jnp.float32) * scale * gain
    return jnp.minimum(jnp.maximum(result, -reach), reach).astype(kind)


def setup_inputs(seed: int = 0) -> dict:
    key_of = jax.random.split(jax.random.key(seed), 7)
    queries = draw_queries(jax.random.fold_in(key_of[6], 71), 0)
    keys = draw_keys(jax.random.fold_in(key_of[6], 71), 0)
    values = scatter_about(key_of[2], (SECTIONS, SEQ, KVH * HD), 1.0, 6.0, ((0, 16), (1, 8), (2, 4)))
    residual = scatter_about(key_of[3], (SECTIONS, SEQ, D), 0.3, 1.796875, ((0, 16), (1, 8), (2, 4)))
    rand_blocks = draw_rand_blocks(jax.random.fold_in(key_of[6], 71), 0)
    block_order = jax.vmap(lambda own: jax.random.permutation(own, NBLK))(jax.random.split(key_of[5], SECTIONS)).reshape((SECTIONS, NBLK)).astype(jnp.int32)
    return {"queries": queries, "keys": keys, "values": values, "residual": residual, "rand_blocks": rand_blocks, "block_order": block_order}


MASKED = -1e+30

def block_rules(query_seq, key_seq, random_rows):
    nearby = key_seq[None, :] >= query_seq[:, None] - 2
    global_keys = key_seq[None, :] < 2
    drawn_keys = jnp.any(random_rows[:, :, None] == key_seq[None, None, :], axis=1)
    return nearby | global_keys | drawn_keys

def token_rules(block_ok, query_seq, key_seq, block_width):
    offsets = jnp.arange(block_width, dtype=jnp.int32)
    query_pos = (query_seq[:, None] * block_width + offsets[None, :]).reshape(-1)
    key_pos = (key_seq[:, None] * block_width + offsets[None, :]).reshape(-1)
    causal = key_pos[None, :] <= query_pos[:, None]
    spread = jnp.repeat(jnp.repeat(block_ok, block_width, axis=0), block_width, axis=1)
    return causal & spread

def section_attention(section_inputs):
    queries_s, keys_s, values_s, random_s, order_s = section_inputs
    groups = HQ // KVH
    keys_f = keys_s.astype(jnp.float32).reshape(SEQ, KVH, HD)
    values_f = values_s.astype(jnp.float32).reshape(SEQ, KVH, HD)
    factor = 1.0 / math.sqrt(HD)

    def one_block(block_index):
        query_seq = lax.dynamic_slice_in_dim(order_s, block_index, 1)
        query_tile = lax.dynamic_slice_in_dim(queries_s, block_index * BLOCK, BLOCK, 0)
        query_tile = query_tile.astype(jnp.float32).reshape(BLOCK, KVH, groups, HD)
        random_rows = lax.dynamic_slice_in_dim(random_s, query_seq[0], 1, 0)
        block_ok = block_rules(query_seq, order_s, random_rows)
        allowed = token_rules(block_ok, query_seq, order_s, BLOCK)[:, None, None, :]
        scores = jnp.einsum('qkgd,rkd->qkgr', query_tile, keys_f) * factor
        scores = jnp.where(allowed, scores, MASKED)
        row_max = lax.optimization_barrier(jnp.max(scores, axis=-1, keepdims=True))
        weights = jnp.where(allowed, jnp.exp(scores - row_max), 0.0)
        row_total = lax.optimization_barrier(jnp.sum(weights, axis=-1))
        rounded = lax.optimization_barrier(weights.astype(jnp.bfloat16)).astype(jnp.float32)
        mixed = jnp.einsum('qkgr,rkd->qkgd', rounded, values_f) / row_total[..., None]
        return mixed.reshape(BLOCK, HQ * HD).astype(jnp.bfloat16)
    outputs = lax.map(one_block, jnp.arange(NBLK, dtype=jnp.int32))
    return outputs.reshape(SEQ, HQ * HD)

def reference(queries, keys, values, residual, rand_blocks, block_order):
    attended = lax.map(section_attention, (queries, keys, values, rand_blocks, block_order))
    summed = (attended.astype(jnp.float32) + residual.astype(jnp.float32)).astype(jnp.bfloat16)
    return jnp.roll(summed, 1, axis=0)
```

```python
import functools
import math

import jax
import jax.numpy as jnp
from jax import lax
from jax.experimental import pallas as pl
from jax.experimental.pallas import tpu as pltpu
from jax.sharding import PartitionSpec as P

MESH = pl.DeviceIdType.MESH
HD = 128
BLOCK = 128
SLOTS = 8
MASKED = -1e30
CHUNKS = 8
HEADS = 4
SIDES = 2
LEFT0, LEFT1, RIGHT1, RIGHT0, SIB, OPP0, OPP1, SIB_LEFT, SIB_RIGHT, SIB_OPP0, SIB_OPP1 = range(11)
PIECES = 11
MID_LAST = False


def kernel(
    zs, ys, q_hbm, k_hbm, v_hbm, r_hbm, rand_ref, order_ref, out_ref,
    kv0, kv1, q_v, r_v, o_v, ksel, vsel, relay, slot_at, slot_ok,
    load_sem, piece_send, piece_recv, out_send, out_recv, mid_recv, mid_send,
):
    kv = (kv0, kv1)
    section, ctx, tp = lax.axis_index("section"), lax.axis_index("ctx"), lax.axis_index("tp")
    tps = ys // 2
    chips = lax.axis_size("ctx") // 2
    z, y = section % zs, (section // zs) * tps + tp
    x, core = ctx // 2, ctx % 2
    left, right = (x + chips - 1) % chips, (x + 1) % chips
    opp = (x + 2) % chips

    def at(chip, c):
        return chip * 2 + c

    def dev_ctx(chip, c):
        return (section, at(chip, c), tp)

    def dev_yz(y2, z2):
        y2 = (y2 + ys) % ys
        return ((y2 // tps) * zs + z2, ctx, y2 % tps)

    sib_dev, left_dev, right_dev = dev_ctx(x, 1 - core), dev_ctx(left, core), dev_ctx(right, core)
    first, last = z == 0, z == zs - 1
    mid = last if MID_LAST else first
    mid_z = zs - 1 if MID_LAST else 0

    own = pl.ds(2 * ctx, 2)
    kv_loads = []
    for h in range(2):
        cols = pl.ds(h * HD, HD)
        for which, src in enumerate((k_hbm, v_hbm)):
            kv_loads.append(
                pltpu.make_async_copy(src.at[:, :, cols], kv[h].at[own, which], load_sem.at[2 * h + which])
            )
    q_load = pltpu.make_async_copy(q_hbm, q_v, load_sem.at[4])
    r_load = pltpu.make_async_copy(r_hbm, r_v, load_sem.at[5])
    for copy in (*kv_loads, q_load, r_load):
        copy.start()

    barrier = pltpu.get_barrier_semaphore()

    def greet(dev):
        pl.semaphore_signal(barrier, inc=1, device_id=dev, device_id_type=MESH)

    greet(sib_dev)
    greet(left_dev)
    greet(right_dev)

    @pl.when(z > 0)
    def _():
        greet((section - 1, ctx, tp))

    if MID_LAST:
        @pl.when(first)
        def _():
            greet(dev_yz(y + 2, zs - 1))
            greet(dev_yz(y - 2, zs - 1))

        @pl.when(last)
        def _():
            greet(dev_yz(y + 2, zs - 1))
            greet(dev_yz(y - 2, zs - 1))
    else:
        @pl.when(first)
        def _():
            greet(dev_yz(y + 2, zs - 1))
            greet(dev_yz(y - 2, zs - 1))
            greet(dev_yz(y + 2, 0))
            greet(dev_yz(y - 2, 0))

    for here, count in ((first, 4 if MID_LAST else 6), (last, 7 if MID_LAST else 5), (~first & ~last, 4)):
        @pl.when(here)
        def _(count=count):
            pl.semaphore_wait(barrier, count)

    def piece(h, tag, blocks, dev):
        part = kv[h].at[blocks]
        return pltpu.make_async_remote_copy(
            src_ref=part, dst_ref=part, send_sem=piece_send.at[h, tag], recv_sem=piece_recv.at[h, tag],
            device_id=dev, device_id_type=MESH,
        )

    def one(chip, c, b):
        return pl.ds(2 * at(chip, c) + b, 1)

    def two(chip, c):
        return pl.ds(2 * at(chip, c), 2)

    sent = {
        LEFT0: (one(x, core, 0), right_dev),
        LEFT1: (one(x, core, 1), right_dev),
        RIGHT1: (one(x, core, 1), left_dev),
        RIGHT0: (one(x, core, 0), left_dev),
        SIB: (two(x, core), sib_dev),
        OPP0: (one(left, core, 0), right_dev),
        OPP1: (one(right, core, 1), left_dev),
        SIB_LEFT: (two(left, core), sib_dev),
        SIB_RIGHT: (two(right, core), sib_dev),
        SIB_OPP0: (one(opp, core, 0), sib_dev),
        SIB_OPP1: (one(opp, core, 1), sib_dev),
    }
    received = {
        LEFT0: (one(left, core, 0), right_dev),
        LEFT1: (one(left, core, 1), right_dev),
        RIGHT1: (one(right, core, 1), left_dev),
        RIGHT0: (one(right, core, 0), left_dev),
        SIB: (two(x, 1 - core), sib_dev),
        OPP0: (one(opp, core, 0), right_dev),
        OPP1: (one(opp, core, 1), left_dev),
        SIB_LEFT: (two(left, 1 - core), sib_dev),
        SIB_RIGHT: (two(right, 1 - core), sib_dev),
        SIB_OPP0: (one(opp, 1 - core, 0), sib_dev),
        SIB_OPP1: (one(opp, 1 - core, 1), sib_dev),
    }

    def send(h, tag):
        return piece(h, tag, *sent[tag])

    def await_piece(h, tag):
        piece(h, tag, *received[tag]).wait_recv()

    def send_own(h):
        for tag in (LEFT0, RIGHT1, LEFT1, RIGHT0, SIB):
            send(h, tag).start()

    def send_far(h):
        await_piece(h, LEFT0)
        send(h, OPP0).start()
        await_piece(h, RIGHT1)
        send(h, OPP1).start()

    def send_sib(h):
        await_piece(h, LEFT1)
        send(h, SIB_LEFT).start()
        await_piece(h, RIGHT0)
        send(h, SIB_RIGHT).start()
        await_piece(h, OPP0)
        send(h, SIB_OPP0).start()
        await_piece(h, OPP1)
        send(h, SIB_OPP1).start()

    def arrive(h):
        for tag in (SIB, SIB_LEFT, SIB_RIGHT, SIB_OPP0, SIB_OPP1):
            await_piece(h, tag)

    kv_loads[0].wait()
    kv_loads[1].wait()
    send_own(0)
    kv_loads[2].wait()
    kv_loads[3].wait()

    for b in range(2):
        i = order_ref[0, 2 * ctx + b]
        rand = [rand_ref[r, 0, i] for r in range(3)]
        wanted = [i, i - 1, i - 2, 0, 1, *rand]
        far = [(rand[r] < i - 2) & (rand[r] >= 2) for r in range(3)]
        valid = [
            i >= 0, i >= 1, i >= 2, i >= 3, i >= 4,
            far[0], far[1] & (rand[1] != rand[0]), far[2] & (rand[2] != rand[0]) & (rand[2] != rand[1]),
        ]
        places = [jnp.int32(0)] * SLOTS
        for p in range(16):
            held = order_ref[0, p]
            places = [jnp.where(held == j, p, place) for j, place in zip(wanted, places)]
        for s in range(SLOTS):
            slot_at[b, s] = places[s]
            slot_ok[b, s] = jnp.where(valid[s], 1, 0)

    send_far(0)
    send_own(1)
    send_sib(0)
    q_load.wait()
    arrive(0)
    r_load.wait()

    def pick(h):
        for b in range(2):
            for s in range(SLOTS):
                place = slot_at[b, s]
                ksel[b, pl.ds(s * BLOCK, BLOCK), :] = kv[h][place, 0]
                vsel[b, pl.ds(s * BLOCK, BLOCK), :] = kv[h][place, 1]

    scale = math.log2(math.e) / math.sqrt(HD)

    def where_out(c, d):
        h, b, half = c // 4, (c // 2) % 2, c % 2
        cols = (h * 2 + half) * (HEADS * HD) + d * (HEADS * HD // 2)
        return pl.ds(pl.multiple_of(b * BLOCK, BLOCK), BLOCK), pl.ds(pl.multiple_of(cols, 2 * HD), 2 * HD)

    def to_next(c, d):
        rows, cols = where_out(c, d)
        return pltpu.make_async_remote_copy(
            src_ref=o_v.at[rows, cols], dst_ref=out_ref.at[rows, cols],
            send_sem=out_send.at[c, d], recv_sem=out_recv.at[c, d],
            device_id=(section + 1, ctx, tp), device_id_type=MESH,
        )

    def to_mid(c, d):
        rows, cols = where_out(c, d)
        return pltpu.make_async_remote_copy(
            src_ref=o_v.at[rows, cols], dst_ref=relay.at[d, c],
            send_sem=out_send.at[c, d], recv_sem=mid_recv.at[c, d],
            device_id=dev_yz(y + 2 - 4 * d, mid_z), device_id_type=MESH,
        )

    def from_mid(c, d):
        rows, cols = where_out(c, d)
        return pltpu.make_async_remote_copy(
            src_ref=relay.at[d, c], dst_ref=out_ref.at[rows, cols],
            send_sem=mid_send.at[c, d], recv_sem=out_recv.at[c, d],
            device_id=dev_yz(y + 2 - 4 * d, 0), device_id_type=MESH,
        )

    def pass_on(c):
        for d in range(SIDES):
            to_mid(c, d).wait_recv()
            from_mid(c, d).start()

    def chunk(c, carry):
        h, b, half = c // 4, (c // 2) % 2, c % 2

        @pl.when(c == 0)
        def _():
            pick(0)

        @pl.when(c == 1)
        def _():
            send_far(1)

        @pl.when(c == 2)
        def _():
            send_sib(1)

        @pl.when(c == 4)
        def _():
            arrive(1)
            pick(1)

        rows = pl.ds(pl.multiple_of(b * BLOCK, BLOCK), BLOCK)
        start = (h * 2 + half) * (HEADS * HD)
        cols = [pl.ds(pl.multiple_of(start + g * HD, HD), HD) for g in range(HEADS)]
        keys, vals = ksel[b], vsel[b]
        bias = [jnp.where(slot_ok[b, s] > 0, 0.0, MASKED) for s in range(SLOTS)]
        row_at = lax.broadcasted_iota(jnp.int32, (BLOCK, BLOCK), 0)
        key_at = lax.broadcasted_iota(jnp.int32, (BLOCK, BLOCK), 1)
        causal = key_at <= row_at
        for g in range(HEADS):
            scores = lax.dot_general(
                q_v[rows, cols[g]], keys, (((1,), (1,)), ((), ())), preferred_element_type=jnp.float32
            )
            parts = [scores[:, s * BLOCK : (s + 1) * BLOCK] for s in range(SLOTS)]
            parts = [jnp.where(causal, parts[0], MASKED)] + [parts[s] + bias[s] for s in range(1, SLOTS)]
            top = functools.reduce(jnp.maximum, parts)
            top = jnp.max(top, axis=1, keepdims=True)
            weights = [jnp.exp2((part - top) * scale) for part in parts]
            total = jnp.sum(functools.reduce(jnp.add, weights), axis=1, keepdims=True)
            packed = jnp.concatenate([w.astype(jnp.bfloat16) for w in weights], axis=1)
            mixed = jnp.dot(packed, vals, preferred_element_type=jnp.float32) / total
            attended = mixed.astype(jnp.bfloat16).astype(jnp.float32)
            o_v[rows, cols[g]] = (attended + r_v[rows, cols[g]].astype(jnp.float32)).astype(jnp.bfloat16)

        @pl.when(z < zs - 1)
        def _():
            for d in range(SIDES):
                to_next(c, d).start()

        @pl.when(last)
        def _():
            for d in range(SIDES):
                to_mid(c, d).start()

        @pl.when(mid & (c >= 6))
        def _():
            pass_on(c - 6)

        return carry

    lax.fori_loop(0, CHUNKS, chunk, 0)

    @pl.when(mid)
    def _():
        def later(c, carry):
            pass_on(c)
            return carry

        lax.fori_loop(2, CHUNKS, later, 0)

    def finish(c, carry):
        for d in range(SIDES):
            to_next(c, d).wait_recv()
            to_next(c, d).wait_send()
        return carry

    lax.fori_loop(0, CHUNKS, finish, 0)

    @pl.when(mid)
    def _():
        def passed(c, carry):
            for d in range(SIDES):
                from_mid(c, d).wait_send()
            return carry

        lax.fori_loop(0, CHUNKS, passed, 0)

    for h in range(2):
        for tag in range(PIECES):
            send(h, tag).wait_send()


def solution(mesh):
    zs = mesh.shape["section"] // 2
    ys = mesh.shape["tp"] * 2

    def body(queries, keys, values, residual, rand_blocks, block_order):
        _, rows, width = queries.shape
        kv_width = keys.shape[2]
        hbm, smem = pl.BlockSpec(memory_space=pl.ANY), pl.BlockSpec(memory_space=pltpu.SMEM)
        blocks = 2 * mesh.shape["ctx"]
        dma = pltpu.SemaphoreType.DMA
        out = pl.pallas_call(
            functools.partial(kernel, zs, ys),
            out_shape=jax.ShapeDtypeStruct((rows, width), jnp.bfloat16),
            in_specs=[hbm, hbm, hbm, hbm, smem, smem],
            out_specs=hbm,
            scratch_shapes=[
                pltpu.VMEM((blocks, 2, BLOCK, HD), jnp.bfloat16),
                pltpu.VMEM((blocks, 2, BLOCK, HD), jnp.bfloat16),
                pltpu.VMEM((rows, width), jnp.bfloat16),
                pltpu.VMEM((rows, width), jnp.bfloat16),
                pltpu.VMEM((rows, width), jnp.bfloat16),
                pltpu.VMEM((2, SLOTS * BLOCK, HD), jnp.bfloat16),
                pltpu.VMEM((2, SLOTS * BLOCK, HD), jnp.bfloat16),
                pltpu.VMEM((SIDES, CHUNKS, BLOCK, 2 * HD), jnp.bfloat16),
                pltpu.SMEM((2, SLOTS), jnp.int32),
                pltpu.SMEM((2, SLOTS), jnp.int32),
                dma((6,)),
                dma((2, PIECES)),
                dma((2, PIECES)),
                dma((CHUNKS, SIDES)),
                dma((CHUNKS, SIDES)),
                dma((CHUNKS, SIDES)),
                dma((CHUNKS, SIDES)),
            ],
            compiler_params=pltpu.CompilerParams(
                collective_id=0, has_side_effects=True, vmem_limit_bytes=56 * 1024 * 1024
            ),
        )(
            queries.reshape(rows, width),
            keys.reshape(rows // BLOCK, BLOCK, kv_width),
            values.reshape(rows // BLOCK, BLOCK, kv_width),
            residual.reshape(rows, width),
            rand_blocks.transpose(2, 0, 1),
            block_order,
        )
        return out.reshape(1, rows, width)

    spec = P("section", "ctx", "tp")
    return jax.shard_map(
        body,
        mesh=mesh,
        in_specs=(spec, spec, spec, spec, P("section", None, None), P("section", None)),
        out_specs=spec,
        check_vma=False,
    )
```

```python
import functools
import math

import jax
import jax.numpy as jnp
from jax import lax
from jax.experimental import pallas as pl
from jax.experimental.pallas import tpu as pltpu
from jax.sharding import PartitionSpec as P

MESH = pl.DeviceIdType.MESH
HD = 128
BLOCK = 128
SLOTS = 8
MASKED = -1e30
CHUNKS = 8
HEADS = 4
SIDES = 2
LEFT0, LEFT1, RIGHT1, RIGHT0, SIB, OPP0, OPP1, SIB_LEFT, SIB_RIGHT, SIB_OPP0, SIB_OPP1 = range(11)
PIECES = 11
HIGH, LOW = 5, 2


def back(way):
    return ((0, HIGH), (2 * way, LOW), (4 * way, 0))


def turn(way):
    return ((2 * way, 0), (4 * way, 0))


def paths_of_units():
    down, up = turn(1), turn(-1)
    pairs = [
        (back(1), down), (back(-1), up), (back(1), down), (back(-1), up),
        (back(1), down), (back(-1), up), (down, up), (down, up),
    ]
    return {(c, d): pairs[c][d] for c in range(CHUNKS) for d in range(SIDES)}


PATHS = paths_of_units()
EARLY = {HIGH: 4}


def hands_on(plane):
    return [
        (c, d, path[i], path[i + 1], i + 2 == len(path))
        for (c, d), path in PATHS.items()
        for i in range(len(path) - 1)
        if path[i][1] == plane
    ]


def legs(plane, last):
    out = [(there[0] - here[0], there[1]) for _, _, here, there, _ in hands_on(plane)]
    if plane == last:
        out += [path[0] for path in PATHS.values()]
    return sorted(set(out))

def kernel(
    zs, ys, q_hbm, k_hbm, v_hbm, r_hbm, rand_ref, order_ref, out_ref,
    kv0, kv1, q_v, r_v, o_v, ksel, vsel, relay, slot_at, slot_ok,
    load_sem, piece_send, piece_recv, out_send, out_recv, mid_recv, mid_send,
):
    kv = (kv0, kv1)
    section, ctx, tp = lax.axis_index("section"), lax.axis_index("ctx"), lax.axis_index("tp")
    tps = ys // 2
    chips = lax.axis_size("ctx") // 2
    z, y = section % zs, (section // zs) * tps + tp
    x, core = ctx // 2, ctx % 2
    left, right = (x + chips - 1) % chips, (x + 1) % chips
    opp = (x + 2) % chips

    def at(chip, c):
        return chip * 2 + c

    def dev_ctx(chip, c):
        return (section, at(chip, c), tp)

    def dev_yz(y2, z2):
        y2 = (y2 + ys) % ys
        return ((y2 // tps) * zs + z2, ctx, y2 % tps)

    sib_dev, left_dev, right_dev = dev_ctx(x, 1 - core), dev_ctx(left, core), dev_ctx(right, core)
    first, last = z == 0, z == zs - 1
    own = pl.ds(2 * ctx, 2)
    kv_loads = []
    for h in range(2):
        cols = pl.ds(h * HD, HD)
        for which, src in enumerate((k_hbm, v_hbm)):
            kv_loads.append(
                pltpu.make_async_copy(src.at[:, :, cols], kv[h].at[own, which], load_sem.at[2 * h + which])
            )
    q_load = pltpu.make_async_copy(q_hbm, q_v, load_sem.at[4])
    r_load = pltpu.make_async_copy(r_hbm, r_v, load_sem.at[5])
    for copy in (*kv_loads, q_load, r_load):
        copy.start()

    barrier = pltpu.get_barrier_semaphore()

    def greet(dev):
        pl.semaphore_signal(barrier, inc=1, device_id=dev, device_id_type=MESH)

    greet(sib_dev)
    greet(left_dev)
    greet(right_dev)

    @pl.when(z > 0)
    def _():
        greet((section - 1, ctx, tp))

    for plane in range(zs):
        sources = [(step, source) for source in range(zs) for step, target in legs(source, zs - 1) if target == plane]
        count = 3 + (plane < zs - 1) + len(legs(plane, zs - 1))

        @pl.when(z == plane)
        def _(sources=sources, count=count):
            for step, source in sources:
                greet(dev_yz(y - step, source))
            pl.semaphore_wait(barrier, count)

    def piece(h, tag, blocks, dev):
        part = kv[h].at[blocks]
        return pltpu.make_async_remote_copy(
            src_ref=part, dst_ref=part, send_sem=piece_send.at[h, tag], recv_sem=piece_recv.at[h, tag],
            device_id=dev, device_id_type=MESH,
        )

    def one(chip, c, b):
        return pl.ds(2 * at(chip, c) + b, 1)

    def two(chip, c):
        return pl.ds(2 * at(chip, c), 2)

    sent = {
        LEFT0: (one(x, core, 0), right_dev),
        LEFT1: (one(x, core, 1), right_dev),
        RIGHT1: (one(x, core, 1), left_dev),
        RIGHT0: (one(x, core, 0), left_dev),
        SIB: (two(x, core), sib_dev),
        OPP0: (one(left, core, 0), right_dev),
        OPP1: (one(right, core, 1), left_dev),
        SIB_LEFT: (two(left, core), sib_dev),
        SIB_RIGHT: (two(right, core), sib_dev),
        SIB_OPP0: (one(opp, core, 0), sib_dev),
        SIB_OPP1: (one(opp, core, 1), sib_dev),
    }
    received = {
        LEFT0: (one(left, core, 0), right_dev),
        LEFT1: (one(left, core, 1), right_dev),
        RIGHT1: (one(right, core, 1), left_dev),
        RIGHT0: (one(right, core, 0), left_dev),
        SIB: (two(x, 1 - core), sib_dev),
        OPP0: (one(opp, core, 0), right_dev),
        OPP1: (one(opp, core, 1), left_dev),
        SIB_LEFT: (two(left, 1 - core), sib_dev),
        SIB_RIGHT: (two(right, 1 - core), sib_dev),
        SIB_OPP0: (one(opp, 1 - core, 0), sib_dev),
        SIB_OPP1: (one(opp, 1 - core, 1), sib_dev),
    }

    def send(h, tag):
        return piece(h, tag, *sent[tag])

    def await_piece(h, tag):
        piece(h, tag, *received[tag]).wait_recv()

    def send_own(h):
        for tag in (LEFT0, RIGHT1, LEFT1, RIGHT0, SIB):
            send(h, tag).start()

    def send_far(h):
        await_piece(h, LEFT0)
        send(h, OPP0).start()
        await_piece(h, RIGHT1)
        send(h, OPP1).start()

    def send_sib(h):
        await_piece(h, LEFT1)
        send(h, SIB_LEFT).start()
        await_piece(h, RIGHT0)
        send(h, SIB_RIGHT).start()
        await_piece(h, OPP0)
        send(h, SIB_OPP0).start()
        await_piece(h, OPP1)
        send(h, SIB_OPP1).start()

    def arrive(h):
        for tag in (SIB, SIB_LEFT, SIB_RIGHT, SIB_OPP0, SIB_OPP1):
            await_piece(h, tag)

    kv_loads[0].wait()
    kv_loads[1].wait()
    send_own(0)
    kv_loads[2].wait()
    kv_loads[3].wait()

    for b in range(2):
        i = order_ref[0, 2 * ctx + b]
        rand = [rand_ref[r, 0, i] for r in range(3)]
        wanted = [i, i - 1, i - 2, 0, 1, *rand]
        far = [(rand[r] < i - 2) & (rand[r] >= 2) for r in range(3)]
        valid = [
            i >= 0, i >= 1, i >= 2, i >= 3, i >= 4,
            far[0], far[1] & (rand[1] != rand[0]), far[2] & (rand[2] != rand[0]) & (rand[2] != rand[1]),
        ]
        places = [jnp.int32(0)] * SLOTS
        for p in range(16):
            held = order_ref[0, p]
            places = [jnp.where(held == j, p, place) for j, place in zip(wanted, places)]
        for s in range(SLOTS):
            slot_at[b, s] = places[s]
            slot_ok[b, s] = jnp.where(valid[s], 1, 0)

    send_far(0)
    send_own(1)
    send_sib(0)
    q_load.wait()
    arrive(0)
    r_load.wait()

    def pick(h, b):
        token0 = kv[h][slot_at[b, 3], 0, pl.ds(0, 16), :].astype(jnp.float32)[:1]
        spare = jnp.broadcast_to(token0, (BLOCK, HD)).astype(jnp.bfloat16)
        ones, zeros = jnp.ones((BLOCK, HD), jnp.bfloat16), jnp.zeros((BLOCK, HD), jnp.bfloat16)
        for s in range(SLOTS):
            place, rows = slot_at[b, s], pl.ds(s * BLOCK, BLOCK)
            ok = slot_ok[b, s] > 0
            ksel[rows, :] = jnp.where(ok, kv[h][place, 0], spare)
            vsel[rows, pl.ds(0, HD)] = jnp.where(ok, kv[h][place, 1], zeros)
            vsel[rows, pl.ds(HD, HD)] = jnp.where(ok, ones, zeros)

    scale = math.log2(math.e) / math.sqrt(HD)

    def where_out(c, d):
        h, b, half = c // 4, (c // 2) % 2, c % 2
        cols = (h * 2 + half) * (HEADS * HD) + d * (HEADS * HD // 2)
        return pl.ds(pl.multiple_of(b * BLOCK, BLOCK), BLOCK), pl.ds(pl.multiple_of(cols, 2 * HD), 2 * HD)

    def to_next(c, d):
        rows, cols = where_out(c, d)
        return pltpu.make_async_remote_copy(
            src_ref=o_v.at[rows, cols], dst_ref=out_ref.at[rows, cols],
            send_sem=out_send.at[c, d], recv_sem=out_recv.at[c, d],
            device_id=(section + 1, ctx, tp), device_id_type=MESH,
        )

    def unit(c, d, src, dst, send_sem, recv_sem, step, plane):
        return pltpu.make_async_remote_copy(
            src_ref=src, dst_ref=dst, send_sem=send_sem.at[c, d], recv_sem=recv_sem.at[c, d],
            device_id=dev_yz(y + step, plane), device_id_type=MESH,
        )

    def first_leg(c, d):
        path, (rows, cols) = PATHS[c, d], where_out(c, d)
        if len(path) == 1:
            return unit(c, d, o_v.at[rows, cols], out_ref.at[rows, cols], out_send, out_recv, *path[0])
        return unit(c, d, o_v.at[rows, cols], relay.at[c, d], out_send, mid_recv, *path[0])

    def next_leg(c, d, here, there, ends):
        step, plane, (rows, cols) = there[0] - here[0], there[1], where_out(c, d)
        if ends:
            return unit(c, d, relay.at[c, d], out_ref.at[rows, cols], mid_send, out_recv, step, plane)
        return unit(c, d, relay.at[c, d], relay.at[c, d], mid_send, mid_recv, step, plane)

    def hand_on(c, d, here, there, ends):
        unit(c, d, relay.at[c, d], relay.at[c, d], mid_send, mid_recv, 0, 0).wait_recv()
        next_leg(c, d, here, there, ends).start()

    def chunk(c, carry):
        h, b, half = c // 4, (c // 2) % 2, c % 2

        @pl.when(c == 1)
        def _():
            send_far(1)

        @pl.when(c == 2)
        def _():
            send_sib(1)

        @pl.when(c == 4)
        def _():
            arrive(1)

        for key_head in range(2):
            @pl.when((h == key_head) & (half == 0))
            def _(key_head=key_head):
                pick(key_head, b)

        rows = pl.ds(pl.multiple_of(b * BLOCK, BLOCK), BLOCK)
        start = (h * 2 + half) * (HEADS * HD)
        cols = [pl.ds(pl.multiple_of(start + g * HD, HD), HD) for g in range(HEADS)]
        row_at = lax.broadcasted_iota(jnp.int32, (BLOCK, BLOCK), 0)
        key_at = lax.broadcasted_iota(jnp.int32, (BLOCK, BLOCK), 1)
        causal = key_at <= row_at
        keys, vals = ksel[...], vsel[...]
        scores = [
            lax.dot_general(
                q_v[rows, cols[g]], keys, (((1,), (1,)), ((), ())), preferred_element_type=jnp.float32
            )
            for g in range(HEADS)
        ]
        weights = []
        for score in scores:
            parts = [score[:, s * BLOCK : (s + 1) * BLOCK] for s in range(SLOTS)]
            parts[0] = jnp.where(causal, parts[0], MASKED)
            top = jnp.max(functools.reduce(jnp.maximum, parts), axis=1, keepdims=True)
            weights.append(
                jnp.concatenate([jnp.exp2((part - top) * scale).astype(jnp.bfloat16) for part in parts], axis=1)
            )
        for g in range(HEADS):
            mixed = jnp.dot(weights[g], vals, preferred_element_type=jnp.float32)
            attended = (mixed[:, :HD] / mixed[:, HD:]).astype(jnp.bfloat16).astype(jnp.float32)
            o_v[rows, cols[g]] = (attended + r_v[rows, cols[g]].astype(jnp.float32)).astype(jnp.bfloat16)

        @pl.when(z < zs - 1)
        def _():
            for d in range(SIDES):
                to_next(c, d).start()

        for k in range(CHUNKS):
            @pl.when(last & (c == k))
            def _(k=k):
                for d in range(SIDES):
                    first_leg(k, d).start()

        for plane, lag in EARLY.items():
            for move in hands_on(plane):
                if move[0] + lag < CHUNKS:
                    @pl.when((z == plane) & (c == move[0] + lag))
                    def _(move=move):
                        hand_on(*move)

        return carry

    lax.fori_loop(0, CHUNKS, chunk, 0)

    for plane in range(zs):
        moves = [m for m in hands_on(plane) if plane not in EARLY or m[0] + EARLY[plane] >= CHUNKS]
        if moves:
            @pl.when(z == plane)
            def _(moves=moves):
                for move in moves:
                    hand_on(*move)

    def finish(c, carry):
        for d in range(SIDES):
            to_next(c, d).wait_recv()
            to_next(c, d).wait_send()
        return carry

    lax.fori_loop(0, CHUNKS, finish, 0)

    for plane in range(zs):
        if hands_on(plane):
            @pl.when(z == plane)
            def _(plane=plane):
                for move in hands_on(plane):
                    next_leg(*move).wait_send()

    for h in range(2):
        for tag in range(PIECES):
            send(h, tag).wait_send()


def solution(mesh):
    zs = mesh.shape["section"] // 2
    ys = mesh.shape["tp"] * 2

    def body(queries, keys, values, residual, rand_blocks, block_order):
        _, rows, width = queries.shape
        kv_width = keys.shape[2]
        hbm, smem = pl.BlockSpec(memory_space=pl.ANY), pl.BlockSpec(memory_space=pltpu.SMEM)
        blocks = 2 * mesh.shape["ctx"]
        dma = pltpu.SemaphoreType.DMA
        out = pl.pallas_call(
            functools.partial(kernel, zs, ys),
            out_shape=pltpu.VMEM((rows, width), jnp.bfloat16),
            in_specs=[hbm, hbm, hbm, hbm, smem, smem],
            out_specs=pl.BlockSpec(memory_space=pl.ANY),
            scratch_shapes=[
                pltpu.VMEM((blocks, 2, BLOCK, HD), jnp.bfloat16),
                pltpu.VMEM((blocks, 2, BLOCK, HD), jnp.bfloat16),
                pltpu.VMEM((rows, width), jnp.bfloat16),
                pltpu.VMEM((rows, width), jnp.bfloat16),
                pltpu.VMEM((rows, width), jnp.bfloat16),
                pltpu.VMEM((SLOTS * BLOCK, HD), jnp.bfloat16),
                pltpu.VMEM((SLOTS * BLOCK, 2 * HD), jnp.bfloat16),
                pltpu.VMEM((CHUNKS, SIDES, BLOCK, 2 * HD), jnp.bfloat16),
                pltpu.SMEM((2, SLOTS), jnp.int32),
                pltpu.SMEM((2, SLOTS), jnp.int32),
                dma((6,)),
                dma((2, PIECES)),
                dma((2, PIECES)),
                dma((CHUNKS, SIDES)),
                dma((CHUNKS, SIDES)),
                dma((CHUNKS, SIDES)),
                dma((CHUNKS, SIDES)),
            ],
            compiler_params=pltpu.CompilerParams(
                collective_id=0, has_side_effects=True, vmem_limit_bytes=56 * 1024 * 1024
            ),
        )(
            queries.reshape(rows, width),
            keys.reshape(rows // BLOCK, BLOCK, kv_width),
            values.reshape(rows // BLOCK, BLOCK, kv_width),
            residual.reshape(rows, width),
            rand_blocks.transpose(2, 0, 1),
            block_order,
        )
        return out.reshape(1, rows, width)

    spec = P("section", "ctx", "tp")
    return jax.shard_map(
        body,
        mesh=mesh,
        in_specs=(spec, spec, spec, spec, P("section", None, None), P("section", None)),
        out_specs=spec,
        check_vma=False,
    )
```

```python
import functools
import math

import jax
import jax.numpy as jnp
from jax import lax
from jax.experimental import pallas as pl
from jax.experimental.pallas import tpu as pltpu
from jax.sharding import PartitionSpec as P

MESH = pl.DeviceIdType.MESH
HD = 128
BLOCK = 128
SLOTS = 8
MASKED = -1e30
CHUNKS = 8
HEADS = 4
SIDES = 4
LEFT0, LEFT1, RIGHT1, RIGHT0, SIB, OPP0, OPP1, SIB_LEFT, SIB_RIGHT, SIB_OPP0, SIB_OPP1 = range(11)
PIECES = 11
HIGH, LOW = 5, 2


def back(way):
    return ((0, HIGH), (2 * way, LOW), (4 * way, 0))


def turn(way):
    return ((2 * way, 0), (4 * way, 0))


def paths_of_units():
    down, up = turn(1), turn(-1)
    plus, minus = back(1), back(-1)
    both, short = (plus, down, minus, up), (down, up, down, up)
    halves = [[both] * 6 + [short] * 2] * 2
    return [{(c, d): pairs[c][d] for c in range(CHUNKS) for d in range(SIDES)} for pairs in halves]


PATHS = paths_of_units()
HELD = {(7, d): ((6, d),) for d in range(SIDES)}
WAITED = {unit for units in HELD.values() for unit in units}
EARLY = {HIGH: 4}


def hands_on(plane):
    moves = {}
    for half, paths in enumerate(PATHS):
        for (c, d), path in paths.items():
            for i in range(len(path) - 1):
                if path[i][1] == plane:
                    moves.setdefault((c, d, path[i], path[i + 1], i + 2 == len(path)), []).append(half)
    return [(tuple(halves), *move) for move, halves in sorted(moves.items())]


def legs(plane, last):
    out = [(there[0] - here[0], there[1]) for _, _, _, here, there, _ in hands_on(plane)]
    if plane == last:
        out += [path[0] for paths in PATHS for path in paths.values()]
    return sorted(set(out))

def kernel(
    zs, ys, q_hbm, k_hbm, v_hbm, r_hbm, rand_ref, order_ref, out_ref,
    kv0, kv1, q_v, r_v, o_v, ksel, vsel, relay, slot_at, slot_ok,
    load_sem, piece_send, piece_recv, out_send, out_recv, mid_recv, mid_send,
):
    kv = (kv0, kv1)
    section, ctx, tp = lax.axis_index("section"), lax.axis_index("ctx"), lax.axis_index("tp")
    tps = ys // 2
    chips = lax.axis_size("ctx") // 2
    z, y = section % zs, (section // zs) * tps + tp
    x, core = ctx // 2, ctx % 2
    left, right = (x + chips - 1) % chips, (x + 1) % chips
    opp = (x + 2) % chips

    def at(chip, c):
        return chip * 2 + c

    def dev_ctx(chip, c):
        return (section, at(chip, c), tp)

    def dev_yz(y2, z2):
        y2 = (y2 + ys) % ys
        return ((y2 // tps) * zs + z2, ctx, y2 % tps)

    sib_dev, left_dev, right_dev = dev_ctx(x, 1 - core), dev_ctx(left, core), dev_ctx(right, core)
    first, last = z == 0, z == zs - 1
    own = pl.ds(2 * ctx, 2)
    kv_loads = []
    for h in range(2):
        cols = pl.ds(h * HD, HD)
        for which, src in enumerate((k_hbm, v_hbm)):
            kv_loads.append(
                pltpu.make_async_copy(src.at[:, :, cols], kv[h].at[own, which], load_sem.at[2 * h + which])
            )
    q_load = pltpu.make_async_copy(q_hbm, q_v, load_sem.at[4])
    r_load = pltpu.make_async_copy(r_hbm, r_v, load_sem.at[5])
    for copy in (*kv_loads, q_load, r_load):
        copy.start()

    barrier = pltpu.get_barrier_semaphore()

    def greet(dev):
        pl.semaphore_signal(barrier, inc=1, device_id=dev, device_id_type=MESH)

    greet(sib_dev)
    greet(left_dev)
    greet(right_dev)

    @pl.when(z > 0)
    def _():
        greet((section - 1, ctx, tp))

    for plane in range(zs):
        sources = [(step, source) for source in range(zs) for step, target in legs(source, zs - 1) if target == plane]
        count = 3 + (plane < zs - 1) + len(legs(plane, zs - 1))

        @pl.when(z == plane)
        def _(sources=sources, count=count):
            for step, source in sources:
                greet(dev_yz(y - step, source))
            pl.semaphore_wait(barrier, count)

    def piece(h, tag, blocks, dev):
        part = kv[h].at[blocks]
        return pltpu.make_async_remote_copy(
            src_ref=part, dst_ref=part, send_sem=piece_send.at[h, tag], recv_sem=piece_recv.at[h, tag],
            device_id=dev, device_id_type=MESH,
        )

    def one(chip, c, b):
        return pl.ds(2 * at(chip, c) + b, 1)

    def two(chip, c):
        return pl.ds(2 * at(chip, c), 2)

    sent = {
        LEFT0: (one(x, core, 0), right_dev),
        LEFT1: (one(x, core, 1), right_dev),
        RIGHT1: (one(x, core, 1), left_dev),
        RIGHT0: (one(x, core, 0), left_dev),
        SIB: (two(x, core), sib_dev),
        OPP0: (one(left, core, 0), right_dev),
        OPP1: (one(right, core, 1), left_dev),
        SIB_LEFT: (two(left, core), sib_dev),
        SIB_RIGHT: (two(right, core), sib_dev),
        SIB_OPP0: (one(opp, core, 0), sib_dev),
        SIB_OPP1: (one(opp, core, 1), sib_dev),
    }
    received = {
        LEFT0: (one(left, core, 0), right_dev),
        LEFT1: (one(left, core, 1), right_dev),
        RIGHT1: (one(right, core, 1), left_dev),
        RIGHT0: (one(right, core, 0), left_dev),
        SIB: (two(x, 1 - core), sib_dev),
        OPP0: (one(opp, core, 0), right_dev),
        OPP1: (one(opp, core, 1), left_dev),
        SIB_LEFT: (two(left, 1 - core), sib_dev),
        SIB_RIGHT: (two(right, 1 - core), sib_dev),
        SIB_OPP0: (one(opp, 1 - core, 0), sib_dev),
        SIB_OPP1: (one(opp, 1 - core, 1), sib_dev),
    }

    def send(h, tag):
        return piece(h, tag, *sent[tag])

    def await_piece(h, tag):
        piece(h, tag, *received[tag]).wait_recv()

    def send_own(h):
        for tag in (LEFT0, RIGHT1, LEFT1, RIGHT0, SIB):
            send(h, tag).start()

    def send_far(h):
        await_piece(h, LEFT0)
        send(h, OPP0).start()
        await_piece(h, RIGHT1)
        send(h, OPP1).start()

    def send_near(h):
        await_piece(h, LEFT1)
        send(h, SIB_LEFT).start()
        await_piece(h, RIGHT0)
        send(h, SIB_RIGHT).start()

    def send_opp(h):
        await_piece(h, OPP0)
        send(h, SIB_OPP0).start()
        await_piece(h, OPP1)
        send(h, SIB_OPP1).start()

    def arrive(h):
        for tag in (SIB, SIB_LEFT, SIB_RIGHT, SIB_OPP0, SIB_OPP1):
            await_piece(h, tag)

    kv_loads[0].wait()
    kv_loads[1].wait()
    send_own(0)
    kv_loads[2].wait()
    kv_loads[3].wait()

    for b in range(2):
        i = order_ref[0, 2 * ctx + b]
        rand = [rand_ref[r, 0, i] for r in range(3)]
        wanted = [i, i - 1, i - 2, 0, 1, *rand]
        far = [(rand[r] < i - 2) & (rand[r] >= 2) for r in range(3)]
        valid = [
            i >= 0, i >= 1, i >= 2, i >= 3, i >= 4,
            far[0], far[1] & (rand[1] != rand[0]), far[2] & (rand[2] != rand[0]) & (rand[2] != rand[1]),
        ]
        places = [jnp.int32(0)] * SLOTS
        for p in range(16):
            held = order_ref[0, p]
            places = [jnp.where(held == j, p, place) for j, place in zip(wanted, places)]
        for s in range(SLOTS):
            slot_at[b, s] = places[s]
            slot_ok[b, s] = jnp.where(valid[s], 1, 0)

    send_far(0)
    send_own(1)
    send_near(0)
    send_opp(0)
    q_load.wait()
    arrive(0)
    r_load.wait()

    def pick(h, b):
        token0 = kv[h][slot_at[b, 3], 0, pl.ds(0, 16), :].astype(jnp.float32)[:1]
        spare = jnp.broadcast_to(token0, (BLOCK, HD)).astype(jnp.bfloat16)
        ones, zeros = jnp.ones((BLOCK, HD), jnp.bfloat16), jnp.zeros((BLOCK, HD), jnp.bfloat16)
        for s in range(SLOTS):
            place, rows = slot_at[b, s], pl.ds(s * BLOCK, BLOCK)
            ok = slot_ok[b, s] > 0
            ksel[rows, :] = jnp.where(ok, kv[h][place, 0], spare)
            vsel[rows, pl.ds(0, HD)] = jnp.where(ok, kv[h][place, 1], zeros)
            vsel[rows, pl.ds(HD, HD)] = jnp.where(ok, ones, zeros)

    scale = math.log2(math.e) / math.sqrt(HD)

    def where_out(c, d):
        h, b, half = c // 4, (c // 2) % 2, c % 2
        cols = (h * 2 + half) * (HEADS * HD) + d * HD
        return pl.ds(pl.multiple_of(b * BLOCK, BLOCK), BLOCK), pl.ds(pl.multiple_of(cols, HD), HD)

    def to_next(c, d):
        rows, cols = where_out(c, d)
        return pltpu.make_async_remote_copy(
            src_ref=o_v.at[rows, cols], dst_ref=out_ref.at[rows, cols],
            send_sem=out_send.at[c, d], recv_sem=out_recv.at[c, d],
            device_id=(section + 1, ctx, tp), device_id_type=MESH,
        )

    def unit(c, d, src, dst, send_sem, recv_sem, step, plane):
        return pltpu.make_async_remote_copy(
            src_ref=src, dst_ref=dst, send_sem=send_sem.at[c, d], recv_sem=recv_sem.at[c, d],
            device_id=dev_yz(y + step, plane), device_id_type=MESH,
        )

    def first_leg(half, c, d):
        step, plane = PATHS[half][c, d][0]
        rows, cols = where_out(c, d)
        return unit(c, d, o_v.at[rows, cols], relay.at[c, d], out_send, mid_recv, step, plane)

    def start_units(units):
        for half in range(2):
            @pl.when(y // tps == half)
            def _(half=half):
                for c, d in units:
                    first_leg(half, c, d).start()

    def next_leg(c, d, here, there, ends):
        step, plane, (rows, cols) = there[0] - here[0], there[1], where_out(c, d)
        if ends:
            return unit(c, d, relay.at[c, d], out_ref.at[rows, cols], mid_send, out_recv, step, plane)
        return unit(c, d, relay.at[c, d], relay.at[c, d], mid_send, mid_recv, step, plane)

    def from_halves(halves, here):
        return True if len(halves) == 2 else (y - here[0] + ys) % ys // tps == halves[0]

    def hand_on(halves, c, d, here, there, ends):
        @pl.when(from_halves(halves, here))
        def _():
            unit(c, d, relay.at[c, d], relay.at[c, d], mid_send, mid_recv, 0, 0).wait_recv()
            next_leg(c, d, here, there, ends).start()

    def handed_on(halves, c, d, here, there, ends):
        @pl.when(from_halves(halves, here))
        def _():
            next_leg(c, d, here, there, ends).wait_send()

    def chunk(c, carry):
        h, b, half = c // 4, (c // 2) % 2, c % 2

        @pl.when(c == 1)
        def _():
            send_far(1)

        @pl.when(c == 2)
        def _():
            send_near(1)

        @pl.when(c == 4)
        def _():
            send_opp(1)

        @pl.when(c == 4)
        def _():
            arrive(1)

        for key_head in range(2):
            @pl.when((h == key_head) & (half == 0))
            def _(key_head=key_head):
                pick(key_head, b)

        rows = pl.ds(pl.multiple_of(b * BLOCK, BLOCK), BLOCK)
        start = (h * 2 + half) * (HEADS * HD)
        cols = [pl.ds(pl.multiple_of(start + g * HD, HD), HD) for g in range(HEADS)]
        row_at = lax.broadcasted_iota(jnp.int32, (BLOCK, BLOCK), 0)
        key_at = lax.broadcasted_iota(jnp.int32, (BLOCK, BLOCK), 1)
        causal = key_at <= row_at
        keys, vals = ksel[...], vsel[...]
        scores = [
            lax.dot_general(
                q_v[rows, cols[g]], keys, (((1,), (1,)), ((), ())), preferred_element_type=jnp.float32
            )
            for g in range(HEADS)
        ]
        weights = []
        for score in scores:
            parts = [score[:, s * BLOCK : (s + 1) * BLOCK] for s in range(SLOTS)]
            parts[0] = jnp.where(causal, parts[0], MASKED)
            top = jnp.max(functools.reduce(jnp.maximum, parts), axis=1, keepdims=True)
            weights.append(
                jnp.concatenate([jnp.exp2((part - top) * scale).astype(jnp.bfloat16) for part in parts], axis=1)
            )
        for g in range(HEADS):
            mixed = jnp.dot(weights[g], vals, preferred_element_type=jnp.float32)
            attended = (mixed[:, :HD] / mixed[:, HD:]).astype(jnp.bfloat16).astype(jnp.float32)
            o_v[rows, cols[g]] = (attended + r_v[rows, cols[g]].astype(jnp.float32)).astype(jnp.bfloat16)

        @pl.when(z < zs - 1)
        def _():
            for d in range(SIDES):
                to_next(c, d).start()

        for k in range(CHUNKS):
            @pl.when(last & (c == k))
            def _(k=k):
                start_units([(k, d) for d in range(SIDES) if (k, d) not in HELD])

        for plane, lag in EARLY.items():
            for move in hands_on(plane):
                if move[1] + lag < CHUNKS:
                    @pl.when((z == plane) & (c == move[1] + lag))
                    def _(move=move):
                        hand_on(*move)

        return carry

    lax.fori_loop(0, CHUNKS, chunk, 0)

    @pl.when(last)
    def _():
        for held, units in HELD.items():
            for before in units:
                first_leg(0, *before).wait_send()
            start_units([held])

    for plane in range(zs):
        moves = [m for m in hands_on(plane) if plane not in EARLY or m[1] + EARLY[plane] >= CHUNKS]
        if moves:
            @pl.when(z == plane)
            def _(moves=moves):
                for move in moves:
                    hand_on(*move)

    for c in range(CHUNKS):
        for d in range(SIDES):
            to_next(c, d).wait_recv()
            if (c, d) not in WAITED:
                to_next(c, d).wait_send()

    @pl.when(~last)
    def _():
        for c, d in sorted(WAITED):
            to_next(c, d).wait_send()

    for plane in range(zs):
        if hands_on(plane):
            @pl.when(z == plane)
            def _(plane=plane):
                for move in hands_on(plane):
                    handed_on(*move)

    for h in range(2):
        for tag in range(PIECES):
            send(h, tag).wait_send()


def solution(mesh):
    zs = mesh.shape["section"] // 2
    ys = mesh.shape["tp"] * 2

    def body(queries, keys, values, residual, rand_blocks, block_order):
        _, rows, width = queries.shape
        kv_width = keys.shape[2]
        hbm, smem = pl.BlockSpec(memory_space=pl.ANY), pl.BlockSpec(memory_space=pltpu.SMEM)
        blocks = 2 * mesh.shape["ctx"]
        dma = pltpu.SemaphoreType.DMA
        out = pl.pallas_call(
            functools.partial(kernel, zs, ys),
            out_shape=pltpu.VMEM((rows, width), jnp.bfloat16),
            in_specs=[hbm, hbm, hbm, hbm, smem, smem],
            out_specs=pl.BlockSpec(memory_space=pl.ANY),
            scratch_shapes=[
                pltpu.VMEM((blocks, 2, BLOCK, HD), jnp.bfloat16),
                pltpu.VMEM((blocks, 2, BLOCK, HD), jnp.bfloat16),
                pltpu.VMEM((rows, width), jnp.bfloat16),
                pltpu.VMEM((rows, width), jnp.bfloat16),
                pltpu.VMEM((rows, width), jnp.bfloat16),
                pltpu.VMEM((SLOTS * BLOCK, HD), jnp.bfloat16),
                pltpu.VMEM((SLOTS * BLOCK, 2 * HD), jnp.bfloat16),
                pltpu.VMEM((CHUNKS, SIDES, BLOCK, HD), jnp.bfloat16),
                pltpu.SMEM((2, SLOTS), jnp.int32),
                pltpu.SMEM((2, SLOTS), jnp.int32),
                dma((6,)),
                dma((2, PIECES)),
                dma((2, PIECES)),
                dma((CHUNKS, SIDES)),
                dma((CHUNKS, SIDES)),
                dma((CHUNKS, SIDES)),
                dma((CHUNKS, SIDES)),
            ],
            compiler_params=pltpu.CompilerParams(
                collective_id=0, has_side_effects=True, vmem_limit_bytes=56 * 1024 * 1024
            ),
        )(
            queries.reshape(rows, width),
            keys.reshape(rows // BLOCK, BLOCK, kv_width),
            values.reshape(rows // BLOCK, BLOCK, kv_width),
            residual.reshape(rows, width),
            rand_blocks.transpose(2, 0, 1),
            block_order,
        )
        return out.reshape(1, rows, width)

    spec = P("section", "ctx", "tp")
    return jax.shard_map(
        body,
        mesh=mesh,
        in_specs=(spec, spec, spec, spec, P("section", None, None), P("section", None)),
        out_specs=spec,
        check_vma=False,
    )
```

```python
import functools
import math

import jax
import jax.numpy as jnp
from jax import lax
from jax.experimental import pallas as pl
from jax.experimental.pallas import tpu as pltpu
from jax.sharding import PartitionSpec as P

MESH = pl.DeviceIdType.MESH
HD = 128
BLOCK = 128
SLOTS = 8
MASKED = -1e30
CHUNKS = 8
HEADS = 4
SIDES = 4
LEFT0, LEFT1, RIGHT1, RIGHT0, SIB, OPP0, OPP1, SIB_LEFT, SIB_RIGHT, SIB_OPP0, SIB_OPP1 = range(11)
PIECES = 11
HIGH, LOW = 5, 2


def back(way):
    return ((0, HIGH), (2 * way, LOW), (4 * way, 0))


def turn(way):
    return ((2 * way, 0), (4 * way, 0))


def paths_of_units():
    down, up = turn(1), turn(-1)
    plus, minus = back(1), back(-1)
    both, short = (plus, down, minus, up), (down, up, down, up)
    halves = [[both] * 6 + [short] * 2] * 2
    return [{(c, d): pairs[c][d] for c in range(CHUNKS) for d in range(SIDES)} for pairs in halves]


PATHS = paths_of_units()
HELD = {(7, d): ((6, d),) for d in range(SIDES)}
WAITED = {unit for units in HELD.values() for unit in units}
EARLY = {HIGH: 3}


def hands_on(plane):
    moves = {}
    for half, paths in enumerate(PATHS):
        for (c, d), path in paths.items():
            for i in range(len(path) - 1):
                if path[i][1] == plane:
                    moves.setdefault((c, d, path[i], path[i + 1], i + 2 == len(path)), []).append(half)
    return [(tuple(halves), *move) for move, halves in sorted(moves.items())]


def legs(plane, last):
    out = [(there[0] - here[0], there[1]) for _, _, _, here, there, _ in hands_on(plane)]
    if plane == last:
        out += [path[0] for paths in PATHS for path in paths.values()]
    return sorted(set(out))

def kernel(
    zs, ys, q_hbm, k_hbm, v_hbm, r_hbm, rand_ref, order_ref, out_ref,
    kv0, kv1, q_v, r_v, o_v, ksel, vsel, relay, slot_at, slot_ok,
    load_sem, piece_send, piece_recv, out_send, out_recv, mid_recv, mid_send,
):
    kv = (kv0, kv1)
    section, ctx, tp = lax.axis_index("section"), lax.axis_index("ctx"), lax.axis_index("tp")
    tps = ys // 2
    chips = lax.axis_size("ctx") // 2
    z, y = section % zs, (section // zs) * tps + tp
    x, core = ctx // 2, ctx % 2
    left, right = (x + chips - 1) % chips, (x + 1) % chips
    opp = (x + 2) % chips

    def at(chip, c):
        return chip * 2 + c

    def dev_ctx(chip, c):
        return (section, at(chip, c), tp)

    def dev_yz(y2, z2):
        y2 = (y2 + ys) % ys
        return ((y2 // tps) * zs + z2, ctx, y2 % tps)

    sib_dev, left_dev, right_dev = dev_ctx(x, 1 - core), dev_ctx(left, core), dev_ctx(right, core)
    first, last = z == 0, z == zs - 1
    own = pl.ds(2 * ctx, 2)
    kv_loads = []
    for h in range(2):
        cols = pl.ds(h * HD, HD)
        for which, src in enumerate((k_hbm, v_hbm)):
            kv_loads.append(
                pltpu.make_async_copy(src.at[:, :, cols], kv[h].at[own, which], load_sem.at[2 * h + which])
            )
    q_load = pltpu.make_async_copy(q_hbm, q_v, load_sem.at[4])
    r_load = pltpu.make_async_copy(r_hbm, r_v, load_sem.at[5])
    for copy in (*kv_loads, q_load, r_load):
        copy.start()

    barrier = pltpu.get_barrier_semaphore()

    def greet(dev):
        pl.semaphore_signal(barrier, inc=1, device_id=dev, device_id_type=MESH)

    greet(sib_dev)
    greet(left_dev)
    greet(right_dev)

    @pl.when(z > 0)
    def _():
        greet((section - 1, ctx, tp))

    for plane in range(zs):
        sources = [(step, source) for source in range(zs) for step, target in legs(source, zs - 1) if target == plane]
        count = 3 + (plane < zs - 1) + len(legs(plane, zs - 1))

        @pl.when(z == plane)
        def _(sources=sources, count=count):
            for step, source in sources:
                greet(dev_yz(y - step, source))
            pl.semaphore_wait(barrier, count)

    def piece(h, tag, blocks, dev):
        part = kv[h].at[blocks]
        return pltpu.make_async_remote_copy(
            src_ref=part, dst_ref=part, send_sem=piece_send.at[h, tag], recv_sem=piece_recv.at[h, tag],
            device_id=dev, device_id_type=MESH,
        )

    def one(chip, c, b):
        return pl.ds(2 * at(chip, c) + b, 1)

    def two(chip, c):
        return pl.ds(2 * at(chip, c), 2)

    sent = {
        LEFT0: (one(x, core, 0), right_dev),
        LEFT1: (one(x, core, 1), right_dev),
        RIGHT1: (one(x, core, 1), left_dev),
        RIGHT0: (one(x, core, 0), left_dev),
        SIB: (two(x, core), sib_dev),
        OPP0: (one(left, core, 0), right_dev),
        OPP1: (one(right, core, 1), left_dev),
        SIB_LEFT: (two(left, core), sib_dev),
        SIB_RIGHT: (two(right, core), sib_dev),
        SIB_OPP0: (one(opp, core, 0), sib_dev),
        SIB_OPP1: (one(opp, core, 1), sib_dev),
    }
    received = {
        LEFT0: (one(left, core, 0), right_dev),
        LEFT1: (one(left, core, 1), right_dev),
        RIGHT1: (one(right, core, 1), left_dev),
        RIGHT0: (one(right, core, 0), left_dev),
        SIB: (two(x, 1 - core), sib_dev),
        OPP0: (one(opp, core, 0), right_dev),
        OPP1: (one(opp, core, 1), left_dev),
        SIB_LEFT: (two(left, 1 - core), sib_dev),
        SIB_RIGHT: (two(right, 1 - core), sib_dev),
        SIB_OPP0: (one(opp, 1 - core, 0), sib_dev),
        SIB_OPP1: (one(opp, 1 - core, 1), sib_dev),
    }

    def send(h, tag):
        return piece(h, tag, *sent[tag])

    def await_piece(h, tag):
        piece(h, tag, *received[tag]).wait_recv()

    def send_own(h):
        for tag in (LEFT0, RIGHT1, LEFT1, RIGHT0, SIB):
            send(h, tag).start()

    def send_far(h):
        await_piece(h, LEFT0)
        send(h, OPP0).start()
        await_piece(h, RIGHT1)
        send(h, OPP1).start()

    def send_near(h):
        await_piece(h, LEFT1)
        send(h, SIB_LEFT).start()
        await_piece(h, RIGHT0)
        send(h, SIB_RIGHT).start()

    def send_opp(h):
        await_piece(h, OPP0)
        send(h, SIB_OPP0).start()
        await_piece(h, OPP1)
        send(h, SIB_OPP1).start()

    def arrive(h):
        for tag in (SIB, SIB_LEFT, SIB_RIGHT, SIB_OPP0, SIB_OPP1):
            await_piece(h, tag)

    kv_loads[0].wait()
    kv_loads[1].wait()
    send_own(0)
    kv_loads[2].wait()
    kv_loads[3].wait()

    for b in range(2):
        i = order_ref[0, 2 * ctx + b]
        rand = [rand_ref[r, 0, i] for r in range(3)]
        wanted = [i, i - 1, i - 2, 0, 1, *rand]
        far = [(rand[r] < i - 2) & (rand[r] >= 2) for r in range(3)]
        valid = [
            i >= 0, i >= 1, i >= 2, i >= 3, i >= 4,
            far[0], far[1] & (rand[1] != rand[0]), far[2] & (rand[2] != rand[0]) & (rand[2] != rand[1]),
        ]
        places = [jnp.int32(0)] * SLOTS
        for p in range(16):
            held = order_ref[0, p]
            places = [jnp.where(held == j, p, place) for j, place in zip(wanted, places)]
        for s in range(SLOTS):
            slot_at[b, s] = places[s]
            slot_ok[b, s] = jnp.where(valid[s], 1, 0)

    send_far(0)
    send_own(1)
    send_near(0)
    send_opp(0)
    q_load.wait()
    arrive(0)
    r_load.wait()

    def pick(h, b):
        token0 = kv[h][slot_at[b, 3], 0, pl.ds(0, 16), :].astype(jnp.float32)[:1]
        spare = jnp.broadcast_to(token0, (BLOCK, HD)).astype(jnp.bfloat16)
        ones, zeros = jnp.ones((BLOCK, HD), jnp.bfloat16), jnp.zeros((BLOCK, HD), jnp.bfloat16)
        for s in range(SLOTS):
            place, rows = slot_at[b, s], pl.ds(s * BLOCK, BLOCK)
            ok = slot_ok[b, s] > 0
            ksel[rows, :] = jnp.where(ok, kv[h][place, 0], spare)
            vsel[rows, pl.ds(0, HD)] = jnp.where(ok, kv[h][place, 1], zeros)
            vsel[rows, pl.ds(HD, HD)] = jnp.where(ok, ones, zeros)

    scale = math.log2(math.e) / math.sqrt(HD)

    def where_out(c, d):
        h, b, half = c // 4, (c // 2) % 2, c % 2
        cols = (h * 2 + half) * (HEADS * HD) + d * HD
        return pl.ds(pl.multiple_of(b * BLOCK, BLOCK), BLOCK), pl.ds(pl.multiple_of(cols, HD), HD)

    def to_next(c, d):
        rows, cols = where_out(c, d)
        return pltpu.make_async_remote_copy(
            src_ref=o_v.at[rows, cols], dst_ref=out_ref.at[rows, cols],
            send_sem=out_send.at[c, d], recv_sem=out_recv.at[c, d],
            device_id=(section + 1, ctx, tp), device_id_type=MESH,
        )

    def unit(c, d, src, dst, send_sem, recv_sem, step, plane):
        return pltpu.make_async_remote_copy(
            src_ref=src, dst_ref=dst, send_sem=send_sem.at[c, d], recv_sem=recv_sem.at[c, d],
            device_id=dev_yz(y + step, plane), device_id_type=MESH,
        )

    def first_leg(half, c, d):
        step, plane = PATHS[half][c, d][0]
        rows, cols = where_out(c, d)
        return unit(c, d, o_v.at[rows, cols], relay.at[c, d], out_send, mid_recv, step, plane)

    def start_units(units):
        for half in range(2):
            @pl.when(y // tps == half)
            def _(half=half):
                for c, d in units:
                    first_leg(half, c, d).start()

    def next_leg(c, d, here, there, ends):
        step, plane, (rows, cols) = there[0] - here[0], there[1], where_out(c, d)
        if ends:
            return unit(c, d, relay.at[c, d], out_ref.at[rows, cols], mid_send, out_recv, step, plane)
        return unit(c, d, relay.at[c, d], relay.at[c, d], mid_send, mid_recv, step, plane)

    def from_halves(halves, here):
        return True if len(halves) == 2 else (y - here[0] + ys) % ys // tps == halves[0]

    def hand_on(halves, c, d, here, there, ends):
        @pl.when(from_halves(halves, here))
        def _():
            unit(c, d, relay.at[c, d], relay.at[c, d], mid_send, mid_recv, 0, 0).wait_recv()
            next_leg(c, d, here, there, ends).start()

    def handed_on(halves, c, d, here, there, ends):
        @pl.when(from_halves(halves, here))
        def _():
            next_leg(c, d, here, there, ends).wait_send()

    def chunk(c, carry):
        h, b, half = c // 4, (c // 2) % 2, c % 2

        @pl.when(c == 1)
        def _():
            send_far(1)

        @pl.when(c == 2)
        def _():
            send_near(1)

        @pl.when(c == 4)
        def _():
            send_opp(1)

        @pl.when(c == 4)
        def _():
            arrive(1)

        for key_head in range(2):
            @pl.when((h == key_head) & (half == 0))
            def _(key_head=key_head):
                pick(key_head, b)

        rows = pl.ds(pl.multiple_of(b * BLOCK, BLOCK), BLOCK)
        start = (h * 2 + half) * (HEADS * HD)
        cols = [pl.ds(pl.multiple_of(start + g * HD, HD), HD) for g in range(HEADS)]
        row_at = lax.broadcasted_iota(jnp.int32, (BLOCK, BLOCK), 0)
        key_at = lax.broadcasted_iota(jnp.int32, (BLOCK, BLOCK), 1)
        causal = key_at <= row_at
        keys, vals = ksel[...], vsel[...]
        scores = [
            lax.dot_general(
                q_v[rows, cols[g]], keys, (((1,), (1,)), ((), ())), preferred_element_type=jnp.float32
            )
            for g in range(HEADS)
        ]
        weights = []
        for score in scores:
            parts = [score[:, s * BLOCK : (s + 1) * BLOCK] for s in range(SLOTS)]
            parts[0] = jnp.where(causal, parts[0], MASKED)
            top = jnp.max(functools.reduce(jnp.maximum, parts), axis=1, keepdims=True)
            weights.append(
                jnp.concatenate([jnp.exp2((part - top) * scale).astype(jnp.bfloat16) for part in parts], axis=1)
            )
        for g in range(HEADS):
            mixed = jnp.dot(weights[g], vals, preferred_element_type=jnp.float32)
            attended = (mixed[:, :HD] / mixed[:, HD:]).astype(jnp.bfloat16).astype(jnp.float32)
            o_v[rows, cols[g]] = (attended + r_v[rows, cols[g]].astype(jnp.float32)).astype(jnp.bfloat16)

        @pl.when(z < zs - 1)
        def _():
            for d in range(SIDES):
                to_next(c, d).start()

        for k in range(CHUNKS):
            @pl.when(last & (c == k))
            def _(k=k):
                start_units([(k, d) for d in range(SIDES) if (k, d) not in HELD])

        for plane, lag in EARLY.items():
            for move in hands_on(plane):
                if move[1] + lag < CHUNKS:
                    @pl.when((z == plane) & (c == move[1] + lag))
                    def _(move=move):
                        hand_on(*move)

        return carry

    lax.fori_loop(0, CHUNKS, chunk, 0)

    @pl.when(last)
    def _():
        for held, units in HELD.items():
            for before in units:
                first_leg(0, *before).wait_send()
            start_units([held])

    for plane in range(zs):
        moves = [m for m in hands_on(plane) if plane not in EARLY or m[1] + EARLY[plane] >= CHUNKS]
        if moves:
            @pl.when(z == plane)
            def _(moves=moves):
                for move in moves:
                    hand_on(*move)

    for c in range(CHUNKS):
        for d in range(SIDES):
            to_next(c, d).wait_recv()
            if (c, d) not in WAITED:
                to_next(c, d).wait_send()

    @pl.when(~last)
    def _():
        for c, d in sorted(WAITED):
            to_next(c, d).wait_send()

    for plane in range(zs):
        if hands_on(plane):
            @pl.when(z == plane)
            def _(plane=plane):
                for move in hands_on(plane):
                    handed_on(*move)

    for h in range(2):
        for tag in range(PIECES):
            send(h, tag).wait_send()


def solution(mesh):
    zs = mesh.shape["section"] // 2
    ys = mesh.shape["tp"] * 2

    def body(queries, keys, values, residual, rand_blocks, block_order):
        _, rows, width = queries.shape
        kv_width = keys.shape[2]
        hbm, smem = pl.BlockSpec(memory_space=pl.ANY), pl.BlockSpec(memory_space=pltpu.SMEM)
        blocks = 2 * mesh.shape["ctx"]
        dma = pltpu.SemaphoreType.DMA
        out = pl.pallas_call(
            functools.partial(kernel, zs, ys),
            out_shape=pltpu.VMEM((rows, width), jnp.bfloat16),
            in_specs=[hbm, hbm, hbm, hbm, smem, smem],
            out_specs=pl.BlockSpec(memory_space=pl.ANY),
            scratch_shapes=[
                pltpu.VMEM((blocks, 2, BLOCK, HD), jnp.bfloat16),
                pltpu.VMEM((blocks, 2, BLOCK, HD), jnp.bfloat16),
                pltpu.VMEM((rows, width), jnp.bfloat16),
                pltpu.VMEM((rows, width), jnp.bfloat16),
                pltpu.VMEM((rows, width), jnp.bfloat16),
                pltpu.VMEM((SLOTS * BLOCK, HD), jnp.bfloat16),
                pltpu.VMEM((SLOTS * BLOCK, 2 * HD), jnp.bfloat16),
                pltpu.VMEM((CHUNKS, SIDES, BLOCK, HD), jnp.bfloat16),
                pltpu.SMEM((2, SLOTS), jnp.int32),
                pltpu.SMEM((2, SLOTS), jnp.int32),
                dma((6,)),
                dma((2, PIECES)),
                dma((2, PIECES)),
                dma((CHUNKS, SIDES)),
                dma((CHUNKS, SIDES)),
                dma((CHUNKS, SIDES)),
                dma((CHUNKS, SIDES)),
            ],
            compiler_params=pltpu.CompilerParams(
                collective_id=0, has_side_effects=True, vmem_limit_bytes=56 * 1024 * 1024
            ),
        )(
            queries.reshape(rows, width),
            keys.reshape(rows // BLOCK, BLOCK, kv_width),
            values.reshape(rows // BLOCK, BLOCK, kv_width),
            residual.reshape(rows, width),
            rand_blocks.transpose(2, 0, 1),
            block_order,
        )
        return out.reshape(1, rows, width)

    spec = P("section", "ctx", "tp")
    return jax.shard_map(
        body,
        mesh=mesh,
        in_specs=(spec, spec, spec, spec, P("section", None, None), P("section", None)),
        out_specs=spec,
        check_vma=False,
    )
```

```python
import functools
import math

import jax
import jax.numpy as jnp
from jax import lax
from jax.experimental import pallas as pl
from jax.experimental.pallas import tpu as pltpu
from jax.sharding import PartitionSpec as P

MESH = pl.DeviceIdType.MESH
HD = 128
BLOCK = 128
SLOTS = 8
MASKED = -1e30
CHUNKS = 8
HEADS = 4
SIDES = 4
LEFT0, LEFT1, RIGHT1, RIGHT0, SIB, OPP0, OPP1, SIB_LEFT, SIB_RIGHT, SIB_OPP0, SIB_OPP1 = range(11)
PIECES = 11
HIGH, LOW = 5, 2


def back(way):
    return ((0, HIGH), (2 * way, LOW), (4 * way, 0))


def turn(way):
    return ((2 * way, 0), (4 * way, 0))


def paths_of_units():
    down, up = turn(1), turn(-1)
    plus, minus = back(1), back(-1)
    both, short = (plus, down, minus, up), (down, up, down, up)
    halves = [[both] * 6 + [short] * 2] * 2
    return [{(c, d): pairs[c][d] for c in range(CHUNKS) for d in range(SIDES)} for pairs in halves]


PATHS = paths_of_units()
HELD = {(7, d): ((6, d),) for d in range(SIDES)}
WAITED = {unit for units in HELD.values() for unit in units}
EARLY = {HIGH: 3}


def hands_on(plane):
    moves = {}
    for half, paths in enumerate(PATHS):
        for (c, d), path in paths.items():
            for i in range(len(path) - 1):
                if path[i][1] == plane:
                    moves.setdefault((c, d, path[i], path[i + 1], i + 2 == len(path)), []).append(half)
    return [(tuple(halves), *move) for move, halves in sorted(moves.items())]


def legs(plane, last):
    out = [(there[0] - here[0], there[1]) for _, _, _, here, there, _ in hands_on(plane)]
    if plane == last:
        out += [path[0] for paths in PATHS for path in paths.values()]
    return sorted(set(out))

def kernel(
    zs, ys, q_hbm, k_hbm, v_hbm, r_hbm, rand_ref, order_ref, out_ref,
    kv0, kv1, q_v, r_v, o_v, ksel, vsel, relay, slot_at, slot_ok,
    load_sem, piece_send, piece_recv, out_send, out_recv, mid_recv, mid_send,
):
    kv = (kv0, kv1)
    section, ctx, tp = lax.axis_index("section"), lax.axis_index("ctx"), lax.axis_index("tp")
    tps = ys // 2
    chips = lax.axis_size("ctx") // 2
    z, y = section % zs, (section // zs) * tps + tp
    x, core = ctx // 2, ctx % 2
    left, right = (x + chips - 1) % chips, (x + 1) % chips
    opp = (x + 2) % chips

    def at(chip, c):
        return chip * 2 + c

    def dev_ctx(chip, c):
        return (section, at(chip, c), tp)

    def dev_yz(y2, z2):
        y2 = (y2 + ys) % ys
        return ((y2 // tps) * zs + z2, ctx, y2 % tps)

    sib_dev, left_dev, right_dev = dev_ctx(x, 1 - core), dev_ctx(left, core), dev_ctx(right, core)
    first, last = z == 0, z == zs - 1
    own = pl.ds(2 * ctx, 2)
    kv_loads = []
    for h in range(2):
        cols = pl.ds(h * HD, HD)
        for which, src in enumerate((k_hbm, v_hbm)):
            kv_loads.append(
                pltpu.make_async_copy(src.at[:, :, cols], kv[h].at[own, which], load_sem.at[2 * h + which])
            )
    q_load = pltpu.make_async_copy(q_hbm, q_v, load_sem.at[4])
    r_load = pltpu.make_async_copy(r_hbm, r_v, load_sem.at[5])
    for copy in (*kv_loads, q_load, r_load):
        copy.start()

    barrier = pltpu.get_barrier_semaphore()

    def greet(dev):
        pl.semaphore_signal(barrier, inc=1, device_id=dev, device_id_type=MESH)

    greet(sib_dev)
    greet(left_dev)
    greet(right_dev)

    @pl.when(z > 0)
    def _():
        greet((section - 1, ctx, tp))

    for plane in range(zs):
        sources = [(step, source) for source in range(zs) for step, target in legs(source, zs - 1) if target == plane]
        count = 3 + (plane < zs - 1) + len(legs(plane, zs - 1))

        @pl.when(z == plane)
        def _(sources=sources, count=count):
            for step, source in sources:
                greet(dev_yz(y - step, source))
            pl.semaphore_wait(barrier, count)

    def piece(h, tag, blocks, dev):
        part = kv[h].at[blocks]
        return pltpu.make_async_remote_copy(
            src_ref=part, dst_ref=part, send_sem=piece_send.at[h, tag], recv_sem=piece_recv.at[h, tag],
            device_id=dev, device_id_type=MESH,
        )

    def one(chip, c, b):
        return pl.ds(2 * at(chip, c) + b, 1)

    def two(chip, c):
        return pl.ds(2 * at(chip, c), 2)

    sent = {
        LEFT0: (one(x, core, 0), right_dev),
        LEFT1: (one(x, core, 1), right_dev),
        RIGHT1: (one(x, core, 1), left_dev),
        RIGHT0: (one(x, core, 0), left_dev),
        SIB: (two(x, core), sib_dev),
        OPP0: (one(left, core, 0), right_dev),
        OPP1: (one(right, core, 1), left_dev),
        SIB_LEFT: (two(left, core), sib_dev),
        SIB_RIGHT: (two(right, core), sib_dev),
        SIB_OPP0: (one(opp, core, 0), sib_dev),
        SIB_OPP1: (one(opp, core, 1), sib_dev),
    }
    received = {
        LEFT0: (one(left, core, 0), right_dev),
        LEFT1: (one(left, core, 1), right_dev),
        RIGHT1: (one(right, core, 1), left_dev),
        RIGHT0: (one(right, core, 0), left_dev),
        SIB: (two(x, 1 - core), sib_dev),
        OPP0: (one(opp, core, 0), right_dev),
        OPP1: (one(opp, core, 1), left_dev),
        SIB_LEFT: (two(left, 1 - core), sib_dev),
        SIB_RIGHT: (two(right, 1 - core), sib_dev),
        SIB_OPP0: (one(opp, 1 - core, 0), sib_dev),
        SIB_OPP1: (one(opp, 1 - core, 1), sib_dev),
    }

    def send(h, tag):
        return piece(h, tag, *sent[tag])

    def await_piece(h, tag):
        piece(h, tag, *received[tag]).wait_recv()

    def send_own(h, tags=(LEFT0, RIGHT1, LEFT1, RIGHT0, SIB)):
        for tag in tags:
            send(h, tag).start()

    def send_far(h):
        await_piece(h, LEFT0)
        send(h, OPP0).start()
        await_piece(h, RIGHT1)
        send(h, OPP1).start()

    def send_near(h):
        await_piece(h, LEFT1)
        send(h, SIB_LEFT).start()
        await_piece(h, RIGHT0)
        send(h, SIB_RIGHT).start()

    def send_opp(h):
        await_piece(h, OPP0)
        send(h, SIB_OPP0).start()
        await_piece(h, OPP1)
        send(h, SIB_OPP1).start()

    def arrive(h):
        for tag in (SIB, SIB_LEFT, SIB_RIGHT, SIB_OPP0, SIB_OPP1):
            await_piece(h, tag)

    kv_loads[0].wait()
    kv_loads[1].wait()
    send_own(0)
    kv_loads[2].wait()
    kv_loads[3].wait()

    for b in range(2):
        i = order_ref[0, 2 * ctx + b]
        rand = [rand_ref[r, 0, i] for r in range(3)]
        wanted = [i, i - 1, i - 2, 0, 1, *rand]
        far = [(rand[r] < i - 2) & (rand[r] >= 2) for r in range(3)]
        valid = [
            i >= 0, i >= 1, i >= 2, i >= 3, i >= 4,
            far[0], far[1] & (rand[1] != rand[0]), far[2] & (rand[2] != rand[0]) & (rand[2] != rand[1]),
        ]
        places = [jnp.int32(0)] * SLOTS
        for p in range(16):
            held = order_ref[0, p]
            places = [jnp.where(held == j, p, place) for j, place in zip(wanted, places)]
        for s in range(SLOTS):
            slot_at[b, s] = places[s]
            slot_ok[b, s] = jnp.where(valid[s], 1, 0)

    send_far(0)
    send_own(1, (LEFT0, RIGHT1))
    send_near(0)
    send_own(1, (LEFT1, RIGHT0, SIB))
    send_opp(0)
    q_load.wait()
    arrive(0)
    r_load.wait()

    def pick(h, b):
        token0 = kv[h][slot_at[b, 3], 0, pl.ds(0, 16), :].astype(jnp.float32)[:1]
        spare = jnp.broadcast_to(token0, (BLOCK, HD)).astype(jnp.bfloat16)
        ones, zeros = jnp.ones((BLOCK, HD), jnp.bfloat16), jnp.zeros((BLOCK, HD), jnp.bfloat16)
        for s in range(SLOTS):
            place, rows = slot_at[b, s], pl.ds(s * BLOCK, BLOCK)
            ok = slot_ok[b, s] > 0
            ksel[rows, :] = jnp.where(ok, kv[h][place, 0], spare)
            vsel[rows, pl.ds(0, HD)] = jnp.where(ok, kv[h][place, 1], zeros)
            vsel[rows, pl.ds(HD, HD)] = jnp.where(ok, ones, zeros)

    scale = math.log2(math.e) / math.sqrt(HD)

    def where_out(c, d):
        h, b, half = c // 4, (c // 2) % 2, c % 2
        cols = (h * 2 + half) * (HEADS * HD) + d * HD
        return pl.ds(pl.multiple_of(b * BLOCK, BLOCK), BLOCK), pl.ds(pl.multiple_of(cols, HD), HD)

    def to_next(c, d):
        rows, cols = where_out(c, d)
        return pltpu.make_async_remote_copy(
            src_ref=o_v.at[rows, cols], dst_ref=out_ref.at[rows, cols],
            send_sem=out_send.at[c, d], recv_sem=out_recv.at[c, d],
            device_id=(section + 1, ctx, tp), device_id_type=MESH,
        )

    def unit(c, d, src, dst, send_sem, recv_sem, step, plane):
        return pltpu.make_async_remote_copy(
            src_ref=src, dst_ref=dst, send_sem=send_sem.at[c, d], recv_sem=recv_sem.at[c, d],
            device_id=dev_yz(y + step, plane), device_id_type=MESH,
        )

    def first_leg(half, c, d):
        step, plane = PATHS[half][c, d][0]
        rows, cols = where_out(c, d)
        return unit(c, d, o_v.at[rows, cols], relay.at[c, d], out_send, mid_recv, step, plane)

    def start_units(units):
        for half in range(2):
            @pl.when(y // tps == half)
            def _(half=half):
                for c, d in units:
                    first_leg(half, c, d).start()

    def next_leg(c, d, here, there, ends):
        step, plane, (rows, cols) = there[0] - here[0], there[1], where_out(c, d)
        if ends:
            return unit(c, d, relay.at[c, d], out_ref.at[rows, cols], mid_send, out_recv, step, plane)
        return unit(c, d, relay.at[c, d], relay.at[c, d], mid_send, mid_recv, step, plane)

    def from_halves(halves, here):
        return True if len(halves) == 2 else (y - here[0] + ys) % ys // tps == halves[0]

    def hand_on(halves, c, d, here, there, ends):
        @pl.when(from_halves(halves, here))
        def _():
            unit(c, d, relay.at[c, d], relay.at[c, d], mid_send, mid_recv, 0, 0).wait_recv()
            next_leg(c, d, here, there, ends).start()

    def handed_on(halves, c, d, here, there, ends):
        @pl.when(from_halves(halves, here))
        def _():
            next_leg(c, d, here, there, ends).wait_send()

    def chunk(c, carry):
        h, b, half = c // 4, (c // 2) % 2, c % 2

        @pl.when(c == 1)
        def _():
            send_far(1)

        @pl.when(c == 2)
        def _():
            send_near(1)

        @pl.when(c == 4)
        def _():
            send_opp(1)

        @pl.when(c == 4)
        def _():
            arrive(1)

        for key_head in range(2):
            @pl.when((h == key_head) & (half == 0))
            def _(key_head=key_head):
                pick(key_head, b)

        rows = pl.ds(pl.multiple_of(b * BLOCK, BLOCK), BLOCK)
        start = (h * 2 + half) * (HEADS * HD)
        cols = [pl.ds(pl.multiple_of(start + g * HD, HD), HD) for g in range(HEADS)]
        row_at = lax.broadcasted_iota(jnp.int32, (BLOCK, BLOCK), 0)
        key_at = lax.broadcasted_iota(jnp.int32, (BLOCK, BLOCK), 1)
        causal = key_at <= row_at
        keys, vals = ksel[...], vsel[...]
        scores = [
            lax.dot_general(
                q_v[rows, cols[g]], keys, (((1,), (1,)), ((), ())), preferred_element_type=jnp.float32
            )
            for g in range(HEADS)
        ]
        weights = []
        for score in scores:
            parts = [score[:, s * BLOCK : (s + 1) * BLOCK] for s in range(SLOTS)]
            parts[0] = jnp.where(causal, parts[0], MASKED)
            top = jnp.max(functools.reduce(jnp.maximum, parts), axis=1, keepdims=True)
            weights.append(
                jnp.concatenate([jnp.exp2((part - top) * scale).astype(jnp.bfloat16) for part in parts], axis=1)
            )
        for g in range(HEADS):
            mixed = jnp.dot(weights[g], vals, preferred_element_type=jnp.float32)
            attended = (mixed[:, :HD] / mixed[:, HD:]).astype(jnp.bfloat16).astype(jnp.float32)
            o_v[rows, cols[g]] = (attended + r_v[rows, cols[g]].astype(jnp.float32)).astype(jnp.bfloat16)

        @pl.when(z < zs - 1)
        def _():
            for d in range(SIDES):
                to_next(c, d).start()

        for k in range(CHUNKS):
            @pl.when(last & (c == k))
            def _(k=k):
                start_units([(k, d) for d in range(SIDES) if (k, d) not in HELD])

        for plane, lag in EARLY.items():
            for move in hands_on(plane):
                if move[1] + lag < CHUNKS:
                    @pl.when((z == plane) & (c == move[1] + lag))
                    def _(move=move):
                        hand_on(*move)

        return carry

    lax.fori_loop(0, CHUNKS, chunk, 0)

    @pl.when(last)
    def _():
        for held, units in HELD.items():
            for before in units:
                first_leg(0, *before).wait_send()
            start_units([held])

    for plane in range(zs):
        moves = [m for m in hands_on(plane) if plane not in EARLY or m[1] + EARLY[plane] >= CHUNKS]
        if moves:
            @pl.when(z == plane)
            def _(moves=moves):
                for move in moves:
                    hand_on(*move)

    for h in range(2):
        for tag in range(PIECES):
            send(h, tag).wait_send()

    for c in range(CHUNKS):
        for d in range(SIDES):
            if (c, d) not in WAITED:
                to_next(c, d).wait_send()

    @pl.when(~last)
    def _():
        for c, d in sorted(WAITED):
            to_next(c, d).wait_send()

    for plane in range(zs):
        if hands_on(plane):
            @pl.when(z == plane)
            def _(plane=plane):
                for move in hands_on(plane):
                    handed_on(*move)

    for c in range(CHUNKS):
        for d in range(SIDES):
            to_next(c, d).wait_recv()


def solution(mesh):
    zs = mesh.shape["section"] // 2
    ys = mesh.shape["tp"] * 2

    def body(queries, keys, values, residual, rand_blocks, block_order):
        _, rows, width = queries.shape
        kv_width = keys.shape[2]
        hbm, smem = pl.BlockSpec(memory_space=pl.ANY), pl.BlockSpec(memory_space=pltpu.SMEM)
        blocks = 2 * mesh.shape["ctx"]
        dma = pltpu.SemaphoreType.DMA
        out = pl.pallas_call(
            functools.partial(kernel, zs, ys),
            out_shape=pltpu.VMEM((rows, width), jnp.bfloat16),
            in_specs=[hbm, hbm, hbm, hbm, smem, smem],
            out_specs=pl.BlockSpec(memory_space=pl.ANY),
            scratch_shapes=[
                pltpu.VMEM((blocks, 2, BLOCK, HD), jnp.bfloat16),
                pltpu.VMEM((blocks, 2, BLOCK, HD), jnp.bfloat16),
                pltpu.VMEM((rows, width), jnp.bfloat16),
                pltpu.VMEM((rows, width), jnp.bfloat16),
                pltpu.VMEM((rows, width), jnp.bfloat16),
                pltpu.VMEM((SLOTS * BLOCK, HD), jnp.bfloat16),
                pltpu.VMEM((SLOTS * BLOCK, 2 * HD), jnp.bfloat16),
                pltpu.VMEM((CHUNKS, SIDES, BLOCK, HD), jnp.bfloat16),
                pltpu.SMEM((2, SLOTS), jnp.int32),
                pltpu.SMEM((2, SLOTS), jnp.int32),
                dma((6,)),
                dma((2, PIECES)),
                dma((2, PIECES)),
                dma((CHUNKS, SIDES)),
                dma((CHUNKS, SIDES)),
                dma((CHUNKS, SIDES)),
                dma((CHUNKS, SIDES)),
            ],
            compiler_params=pltpu.CompilerParams(
                collective_id=0, has_side_effects=True, vmem_limit_bytes=56 * 1024 * 1024
            ),
        )(
            queries.reshape(rows, width),
            keys.reshape(rows // BLOCK, BLOCK, kv_width),
            values.reshape(rows // BLOCK, BLOCK, kv_width),
            residual.reshape(rows, width),
            rand_blocks.transpose(2, 0, 1),
            block_order,
        )
        return out.reshape(1, rows, width)

    spec = P("section", "ctx", "tp")
    return jax.shard_map(
        body,
        mesh=mesh,
        in_specs=(spec, spec, spec, spec, P("section", None, None), P("section", None)),
        out_specs=spec,
        check_vma=False,
    )
```

```python
import functools
import math

import jax
import jax.numpy as jnp
from jax import lax
from jax.experimental import pallas as pl
from jax.experimental.pallas import tpu as pltpu
from jax.sharding import PartitionSpec as P

MESH = pl.DeviceIdType.MESH
HD = 128
BLOCK = 128
SLOTS = 8
MASKED = -1e30
CHUNKS = 8
HEADS = 4
SIDES = 4
LEFT0, LEFT1, RIGHT1, RIGHT0, SIB, OPP0, OPP1, SIB_LEFT, SIB_RIGHT, SIB_OPP0, SIB_OPP1 = range(11)
PIECES = 11
HIGH, LOW = 5, 2


def back(way):
    return ((0, HIGH), (2 * way, LOW), (4 * way, 0))


def turn(way):
    return ((2 * way, 0), (4 * way, 0))


def paths_of_units():
    down, up = turn(1), turn(-1)
    plus, minus = back(1), back(-1)
    both, short = (plus, down, minus, up), (down, up, down, up)
    halves = [[both] * 6 + [short] * 2] * 2
    return [{(c, d): pairs[c][d] for c in range(CHUNKS) for d in range(SIDES)} for pairs in halves]


PATHS = paths_of_units()
HELD = {(7, d): ((6, d),) for d in range(SIDES)}
WAITED = {unit for units in HELD.values() for unit in units}
EARLY = {HIGH: 3}


def hands_on(plane):
    moves = {}
    for half, paths in enumerate(PATHS):
        for (c, d), path in paths.items():
            for i in range(len(path) - 1):
                if path[i][1] == plane:
                    moves.setdefault((c, d, path[i], path[i + 1], i + 2 == len(path)), []).append(half)
    return [(tuple(halves), *move) for move, halves in sorted(moves.items())]


def legs(plane, last):
    out = [(there[0] - here[0], there[1]) for _, _, _, here, there, _ in hands_on(plane)]
    if plane == last:
        out += [path[0] for paths in PATHS for path in paths.values()]
    return sorted(set(out))

def kernel(
    zs, ys, q_hbm, k_hbm, v_hbm, r_hbm, rand_ref, order_ref, out_ref,
    kv0, kv1, q_v, r_v, o_v, ksel, vsel, relay, slot_at, slot_ok,
    load_sem, piece_send, piece_recv, out_send, out_recv, mid_recv, mid_send,
):
    kv = (kv0, kv1)
    section, ctx, tp = lax.axis_index("section"), lax.axis_index("ctx"), lax.axis_index("tp")
    tps = ys // 2
    chips = lax.axis_size("ctx") // 2
    z, y = section % zs, (section // zs) * tps + tp
    x, core = ctx // 2, ctx % 2
    left, right = (x + chips - 1) % chips, (x + 1) % chips
    opp = (x + 2) % chips

    def at(chip, c):
        return chip * 2 + c

    def dev_ctx(chip, c):
        return (section, at(chip, c), tp)

    def dev_yz(y2, z2):
        y2 = (y2 + ys) % ys
        return ((y2 // tps) * zs + z2, ctx, y2 % tps)

    sib_dev, left_dev, right_dev = dev_ctx(x, 1 - core), dev_ctx(left, core), dev_ctx(right, core)
    first, last = z == 0, z == zs - 1
    own = pl.ds(2 * ctx, 2)
    kv_loads = []
    for h in range(2):
        cols = pl.ds(h * HD, HD)
        for which, src in enumerate((k_hbm, v_hbm)):
            kv_loads.append(
                pltpu.make_async_copy(src.at[:, :, cols], kv[h].at[own, which], load_sem.at[2 * h + which])
            )
    q_load = pltpu.make_async_copy(q_hbm, q_v, load_sem.at[4])
    r_load = pltpu.make_async_copy(r_hbm, r_v, load_sem.at[5])
    for copy in (*kv_loads, q_load, r_load):
        copy.start()

    barrier = pltpu.get_barrier_semaphore()

    def greet(dev):
        pl.semaphore_signal(barrier, inc=1, device_id=dev, device_id_type=MESH)

    greet(sib_dev)
    greet(left_dev)
    greet(right_dev)

    @pl.when(z > 0)
    def _():
        greet((section - 1, ctx, tp))

    for plane in range(zs):
        sources = [(step, source) for source in range(zs) for step, target in legs(source, zs - 1) if target == plane]
        count = 3 + (plane < zs - 1) + len(legs(plane, zs - 1))

        @pl.when(z == plane)
        def _(sources=sources, count=count):
            for step, source in sources:
                greet(dev_yz(y - step, source))
            pl.semaphore_wait(barrier, count)

    def piece(h, tag, blocks, dev):
        part = kv[h].at[blocks]
        return pltpu.make_async_remote_copy(
            src_ref=part, dst_ref=part, send_sem=piece_send.at[h, tag], recv_sem=piece_recv.at[h, tag],
            device_id=dev, device_id_type=MESH,
        )

    def one(chip, c, b):
        return pl.ds(2 * at(chip, c) + b, 1)

    def two(chip, c):
        return pl.ds(2 * at(chip, c), 2)

    sent = {
        LEFT0: (one(x, core, 0), right_dev),
        LEFT1: (one(x, core, 1), right_dev),
        RIGHT1: (one(x, core, 1), left_dev),
        RIGHT0: (one(x, core, 0), left_dev),
        SIB: (two(x, core), sib_dev),
        OPP0: (one(left, core, 0), right_dev),
        OPP1: (one(right, core, 1), left_dev),
        SIB_LEFT: (two(left, core), sib_dev),
        SIB_RIGHT: (two(right, core), sib_dev),
        SIB_OPP0: (one(opp, core, 0), sib_dev),
        SIB_OPP1: (one(opp, core, 1), sib_dev),
    }
    received = {
        LEFT0: (one(left, core, 0), right_dev),
        LEFT1: (one(left, core, 1), right_dev),
        RIGHT1: (one(right, core, 1), left_dev),
        RIGHT0: (one(right, core, 0), left_dev),
        SIB: (two(x, 1 - core), sib_dev),
        OPP0: (one(opp, core, 0), right_dev),
        OPP1: (one(opp, core, 1), left_dev),
        SIB_LEFT: (two(left, 1 - core), sib_dev),
        SIB_RIGHT: (two(right, 1 - core), sib_dev),
        SIB_OPP0: (one(opp, 1 - core, 0), sib_dev),
        SIB_OPP1: (one(opp, 1 - core, 1), sib_dev),
    }

    def send(h, tag):
        return piece(h, tag, *sent[tag])

    def await_piece(h, tag):
        piece(h, tag, *received[tag]).wait_recv()

    def send_own(h, tags=(LEFT0, RIGHT1, LEFT1, RIGHT0, SIB)):
        for tag in tags:
            send(h, tag).start()

    def send_far(h):
        await_piece(h, LEFT0)
        send(h, OPP0).start()
        await_piece(h, RIGHT1)
        send(h, OPP1).start()

    def send_near(h):
        await_piece(h, LEFT1)
        send(h, SIB_LEFT).start()
        await_piece(h, RIGHT0)
        send(h, SIB_RIGHT).start()

    def send_opp(h):
        await_piece(h, OPP0)
        send(h, SIB_OPP0).start()
        await_piece(h, OPP1)
        send(h, SIB_OPP1).start()

    def arrive(h):
        for tag in (SIB, SIB_LEFT, SIB_RIGHT, SIB_OPP0, SIB_OPP1):
            await_piece(h, tag)

    kv_loads[0].wait()
    kv_loads[1].wait()
    send_own(0)
    kv_loads[2].wait()
    kv_loads[3].wait()

    for b in range(2):
        i = order_ref[0, 2 * ctx + b]
        rand = [rand_ref[r, 0, i] for r in range(3)]
        wanted = [i, i - 1, i - 2, 0, 1, *rand]
        far = [(rand[r] < i - 2) & (rand[r] >= 2) for r in range(3)]
        valid = [
            i >= 0, i >= 1, i >= 2, i >= 3, i >= 4,
            far[0], far[1] & (rand[1] != rand[0]), far[2] & (rand[2] != rand[0]) & (rand[2] != rand[1]),
        ]
        places = [jnp.int32(0)] * SLOTS
        for p in range(16):
            held = order_ref[0, p]
            places = [jnp.where(held == j, p, place) for j, place in zip(wanted, places)]
        for s in range(SLOTS):
            slot_at[b, s] = places[s]
            slot_ok[b, s] = jnp.where(valid[s], 1, 0)

    send_far(0)
    send_own(1, (LEFT0, RIGHT1))
    send_near(0)
    send_own(1, (LEFT1, RIGHT0, SIB))
    send_opp(0)
    q_load.wait()
    arrive(0)
    r_load.wait()

    def pick(h, b):
        token0 = kv[h][slot_at[b, 3], 0, pl.ds(0, 16), :].astype(jnp.float32)[:1]
        spare = jnp.broadcast_to(token0, (BLOCK, HD)).astype(jnp.bfloat16)
        ones, zeros = jnp.ones((BLOCK, HD), jnp.bfloat16), jnp.zeros((BLOCK, HD), jnp.bfloat16)
        for s in range(SLOTS):
            place, rows = slot_at[b, s], pl.ds(s * BLOCK, BLOCK)
            ok = slot_ok[b, s] > 0
            ksel[rows, :] = jnp.where(ok, kv[h][place, 0], spare)
            vsel[rows, pl.ds(0, HD)] = jnp.where(ok, kv[h][place, 1], zeros)
            vsel[rows, pl.ds(HD, HD)] = jnp.where(ok, ones, zeros)

    scale = math.log2(math.e) / math.sqrt(HD)

    def where_out(c, d):
        h, b, half = c // 4, (c // 2) % 2, c % 2
        cols = (h * 2 + half) * (HEADS * HD) + d * HD
        return pl.ds(pl.multiple_of(b * BLOCK, BLOCK), BLOCK), pl.ds(pl.multiple_of(cols, HD), HD)

    def to_next(c, d):
        rows, cols = where_out(c, d)
        return pltpu.make_async_remote_copy(
            src_ref=o_v.at[rows, cols], dst_ref=out_ref.at[rows, cols],
            send_sem=out_send.at[c, d], recv_sem=out_recv.at[c, d],
            device_id=((section + 1) % lax.axis_size("section"), ctx, tp), device_id_type=MESH,
        )

    def unit(c, d, src, dst, send_sem, recv_sem, step, plane):
        return pltpu.make_async_remote_copy(
            src_ref=src, dst_ref=dst, send_sem=send_sem.at[c, d], recv_sem=recv_sem.at[c, d],
            device_id=dev_yz(y + step, plane), device_id_type=MESH,
        )

    def first_leg(half, c, d):
        step, plane = PATHS[half][c, d][0]
        rows, cols = where_out(c, d)
        return unit(c, d, o_v.at[rows, cols], relay.at[c, d], out_send, mid_recv, step, plane)

    def start_units(units):
        for half in range(2):
            @pl.when(y // tps == half)
            def _(half=half):
                for c, d in units:
                    first_leg(half, c, d).start()

    def next_leg(c, d, here, there, ends):
        step, plane, (rows, cols) = there[0] - here[0], there[1], where_out(c, d)
        if ends:
            return unit(c, d, relay.at[c, d], out_ref.at[rows, cols], mid_send, out_recv, step, plane)
        return unit(c, d, relay.at[c, d], relay.at[c, d], mid_send, mid_recv, step, plane)

    def from_halves(halves, here):
        return True if len(halves) == 2 else (y - here[0] + ys) % ys // tps == halves[0]

    def hand_on(halves, c, d, here, there, ends):
        @pl.when(from_halves(halves, here))
        def _():
            unit(c, d, relay.at[c, d], relay.at[c, d], mid_send, mid_recv, 0, 0).wait_recv()
            next_leg(c, d, here, there, ends).start()

    def handed_on(halves, c, d, here, there, ends):
        @pl.when(from_halves(halves, here))
        def _():
            next_leg(c, d, here, there, ends).wait_send()

    def chunk(c, carry):
        h, b, half = c // 4, (c // 2) % 2, c % 2

        @pl.when(c == 1)
        def _():
            send_far(1)

        @pl.when(c == 2)
        def _():
            send_near(1)

        @pl.when(c == 4)
        def _():
            send_opp(1)

        @pl.when(c == 4)
        def _():
            arrive(1)

        for key_head in range(2):
            @pl.when((h == key_head) & (half == 0))
            def _(key_head=key_head):
                pick(key_head, b)

        rows = pl.ds(pl.multiple_of(b * BLOCK, BLOCK), BLOCK)
        start = (h * 2 + half) * (HEADS * HD)
        cols = [pl.ds(pl.multiple_of(start + g * HD, HD), HD) for g in range(HEADS)]
        row_at = lax.broadcasted_iota(jnp.int32, (BLOCK, BLOCK), 0)
        key_at = lax.broadcasted_iota(jnp.int32, (BLOCK, BLOCK), 1)
        causal = key_at <= row_at
        keys, vals = ksel[...], vsel[...]
        scores = [
            lax.dot_general(
                q_v[rows, cols[g]], keys, (((1,), (1,)), ((), ())), preferred_element_type=jnp.float32
            )
            for g in range(HEADS)
        ]
        weights = []
        for score in scores:
            parts = [score[:, s * BLOCK : (s + 1) * BLOCK] for s in range(SLOTS)]
            parts[0] = jnp.where(causal, parts[0], MASKED)
            top = jnp.max(functools.reduce(jnp.maximum, parts), axis=1, keepdims=True)
            weights.append(
                jnp.concatenate([jnp.exp2((part - top) * scale).astype(jnp.bfloat16) for part in parts], axis=1)
            )
        for g in range(HEADS):
            mixed = jnp.dot(weights[g], vals, preferred_element_type=jnp.float32)
            attended = (mixed[:, :HD] / mixed[:, HD:]).astype(jnp.bfloat16).astype(jnp.float32)
            o_v[rows, cols[g]] = (attended + r_v[rows, cols[g]].astype(jnp.float32)).astype(jnp.bfloat16)

        @pl.when(z < zs - 1)
        def _():
            for d in range(SIDES):
                to_next(c, d).start()

        for k in range(CHUNKS):
            @pl.when(last & (c == k))
            def _(k=k):
                start_units([(k, d) for d in range(SIDES) if (k, d) not in HELD])

        for plane, lag in EARLY.items():
            for move in hands_on(plane):
                if move[1] + lag < CHUNKS:
                    @pl.when((z == plane) & (c == move[1] + lag))
                    def _(move=move):
                        hand_on(*move)

        return carry

    lax.fori_loop(0, CHUNKS, chunk, 0)

    @pl.when(last)
    def _():
        for held, units in HELD.items():
            for before in units:
                first_leg(0, *before).wait_send()
            start_units([held])

    for plane in range(zs):
        moves = [m for m in hands_on(plane) if plane not in EARLY or m[1] + EARLY[plane] >= CHUNKS]
        if moves:
            @pl.when(z == plane)
            def _(moves=moves):
                for move in moves:
                    hand_on(*move)

    for h in range(2):
        for tag in range(PIECES):
            send(h, tag).wait_send()

    for c in range(CHUNKS):
        for d in range(SIDES):
            if (c, d) not in WAITED:
                to_next(c, d).wait_send()

    @pl.when(~last)
    def _():
        for c, d in sorted(WAITED):
            to_next(c, d).wait_send()

    for plane in range(zs):
        if hands_on(plane):
            @pl.when(z == plane)
            def _(plane=plane):
                for move in hands_on(plane):
                    handed_on(*move)

    for c in range(CHUNKS):
        for d in range(SIDES):
            to_next(c, d).wait_recv()


def solution(mesh):
    zs = mesh.shape["section"] // 2
    ys = mesh.shape["tp"] * 2

    def body(queries, keys, values, residual, rand_blocks, block_order):
        _, rows, width = queries.shape
        kv_width = keys.shape[2]
        hbm, smem = pl.BlockSpec(memory_space=pl.ANY), pl.BlockSpec(memory_space=pltpu.SMEM)
        blocks = 2 * mesh.shape["ctx"]
        dma = pltpu.SemaphoreType.DMA
        out = pl.pallas_call(
            functools.partial(kernel, zs, ys),
            out_shape=pltpu.VMEM((rows, width), jnp.bfloat16),
            in_specs=[hbm, hbm, hbm, hbm, smem, smem],
            out_specs=pl.BlockSpec(memory_space=pl.ANY),
            scratch_shapes=[
                pltpu.VMEM((blocks, 2, BLOCK, HD), jnp.bfloat16),
                pltpu.VMEM((blocks, 2, BLOCK, HD), jnp.bfloat16),
                pltpu.VMEM((rows, width), jnp.bfloat16),
                pltpu.VMEM((rows, width), jnp.bfloat16),
                pltpu.VMEM((rows, width), jnp.bfloat16),
                pltpu.VMEM((SLOTS * BLOCK, HD), jnp.bfloat16),
                pltpu.VMEM((SLOTS * BLOCK, 2 * HD), jnp.bfloat16),
                pltpu.VMEM((CHUNKS, SIDES, BLOCK, HD), jnp.bfloat16),
                pltpu.SMEM((2, SLOTS), jnp.int32),
                pltpu.SMEM((2, SLOTS), jnp.int32),
                dma((6,)),
                dma((2, PIECES)),
                dma((2, PIECES)),
                dma((CHUNKS, SIDES)),
                dma((CHUNKS, SIDES)),
                dma((CHUNKS, SIDES)),
                dma((CHUNKS, SIDES)),
            ],
            compiler_params=pltpu.CompilerParams(
                collective_id=0, has_side_effects=True, vmem_limit_bytes=56 * 1024 * 1024
            ),
        )(
            queries.reshape(rows, width),
            keys.reshape(rows // BLOCK, BLOCK, kv_width),
            values.reshape(rows // BLOCK, BLOCK, kv_width),
            residual.reshape(rows, width),
            rand_blocks.transpose(2, 0, 1),
            block_order,
        )
        return out.reshape(1, rows, width)

    spec = P("section", "ctx", "tp")
    return jax.shard_map(
        body,
        mesh=mesh,
        in_specs=(spec, spec, spec, spec, P("section", None, None), P("section", None)),
        out_specs=spec,
        check_vma=False,
    )
```
